512 devices in a mesh: cfg: 64 (over y, x, core), tp: 8 (over z).
Axes of the slice: x: 4, y: 8, z: 8, core: 2. Of those that a mesh axis runs over, the one named last changes fastest.
Arguments:
- pool: bfloat16 [64, 192, 8192], P('cfg', None, 'tp'), may hold values from -6 to 6
- base_run: int32 [1], replicated, may hold values from 0 to 63
- gain: bfloat16 [8192], replicated, may hold values from 0.099609375 to 1.8984375
- w_key: bfloat16 [8192, 1024], P(None, 'tp'), may hold values from -0.0625 to 0.0625
- w_value: bfloat16 [8192, 1024], P(None, 'tp'), may hold values from -0.0625 to 0.0625
- w_query: bfloat16 [8192, 8192], P('cfg', 'tp'), may hold values from -0.0625 to 0.0625
- src_pos: int32 [192, 64, 2], P(None, 'cfg'), may hold values from 0 to 191
- dst_pos: int32 [192, 64, 2], P('cfg'), may hold values from 0 to 187, as said below
- counts: int32 [192, 64], P('cfg'), may hold values from 0 to 2
Outputs:
- attended: bfloat16 [192, 4, 8192], P('cfg', None, 'tp')
- keys: bfloat16 [192, 192, 1024], P('cfg', None, 'tp')
- values: bfloat16 [192, 192, 1024], P('cfg', None, 'tp')
The draws below stay inside these ranges and needn't reach their ends.
Inputs may be any that keep to these rules, and one draw needn't show every extreme that they name: `dst_pos`: within one config all 128 entries differ and lie below 188. `counts`: slots of config c and source run s in use, the first ones of the 2.
All inputs are finite; a program needn't handle non-finite values.
Results may differ from the reference program's by a relative error of at most 0.023.
Values may be sent and summed in bfloat16 or wider, within the bound.
A program may use at most 64 MiB of HBM per device.

```python
import math
import jax
import jax.numpy as jnp
from jax import lax

D = 8192
Q_HEADS = 64
KV_HEADS = 8
HD = 128
SEQ = 192
CAP = 2
PROBE = 4
CONFIGS = 192
SOURCES = 64


def draw_dst_pos(key, part):
    key = jax.random.fold_in(key, 11)
    config_keys = jax.random.split(key, CONFIGS)

    def one_config(single_key):
        return jax.random.permutation(single_key, SEQ - PROBE)[:SOURCES * CAP]
    chosen = jax.vmap(one_config)(config_keys)
    return chosen.reshape(CONFIGS, SOURCES, CAP).astype(jnp.int32)


def with_ends(array, stream_key, least, top_value):
    longest = array.shape.index(max(array.shape))
    spots = []
    for shift in (0, 1):
        where = [jax.random.randint(jax.random.fold_in(stream_key, axis), (), 0, length) for axis, length in enumerate(array.shape)]
        where[longest] = (where[longest] + shift) % array.shape[longest]
        spots.append(tuple(where))
    return array.at[spots[0]].set(least).at[spots[1]].set(top_value)


def block_levels(stream_key, shape, cuts, smallest, high):
    def one(dim, blocks):
        draws = jax.random.uniform(jax.random.fold_in(jax.random.fold_in(stream_key, 6), dim), (blocks,), jnp.float32, smallest / len(cuts), high / len(cuts))
        return jnp.repeat(jnp.exp(draws), shape[dim] // blocks).reshape((-1,) + (1,) * (len(shape) - dim - 1))

    factor_of = one(*cuts[0])
    for cut in cuts[1:]:
        factor_of = factor_of * one(*cut)
    return factor_of


def centred(stream_key, dims, scale, limit, shards=(), kind=jnp.bfloat16):
    level = block_levels(stream_key, dims, shards, -0.22, 0.18) if shards else 1.0
    values = jax.random.normal(stream_key, dims, jnp.float32) * scale * level
    return jnp.minimum(jnp.maximum(values, -limit), limit).astype(kind)


def setup_inputs(seed: int = 0) -> dict:
    key_of = jax.random.split(jax.random.key(seed), 10)
    return {
        "pool": centred(key_of[0], (SOURCES, SEQ, D), 1.0, 6.0, ((0, 64), (2, 8))),
        "base_run": jax.random.randint(key_of[1], (1,), 0, SOURCES).astype(jnp.int32),
        "gain": jnp.clip(1.0 + 0.18 * jax.random.normal(key_of[2], (D,), jnp.float32), 0.099609375, 1.8984375).astype(jnp.bfloat16),
        "w_key": centred(key_of[3], (D, KV_HEADS * HD), D ** -0.5, 0.0625, ((1, 8),)),
        "w_value": centred(key_of[4], (D, KV_HEADS * HD), D ** -0.5, 0.0625, ((1, 8),)),
        "w_query": centred(key_of[5], (D, Q_HEADS * HD), D ** -0.5, 0.0625, ((0, 64), (1, 8))),
        "src_pos": with_ends(jax.random.randint(key_of[6], (CONFIGS, SOURCES, CAP), 0, SEQ), jax.random.fold_in(key_of[6], 1), 0, SEQ - 1).astype(jnp.int32),
        "dst_pos": draw_dst_pos(jax.random.fold_in(key_of[9], 71), 0),
        "counts": with_ends(jax.random.randint(key_of[8], (CONFIGS, SOURCES), 0, CAP + 1), jax.random.fold_in(key_of[8], 1), 0, CAP).astype(jnp.int32),
    }


rope_base = 500000.0
epsilon = 1e-05

def rotate(tensor, positions):
    half_dim = tensor.shape[-1] // 2
    inverse_freq = jnp.exp(jnp.arange(half_dim, dtype=jnp.float32) * (-2.0 * math.log(rope_base) / tensor.shape[-1]))
    angles = positions.astype(jnp.float32)[:, None] * inverse_freq[None, :]
    cosine = jnp.cos(angles)[:, None, :]
    sine_vals = jnp.sin(angles)[:, None, :]
    lower_half = tensor[..., :half_dim]
    upper_half = tensor[..., half_dim:]
    return jnp.concatenate([lower_half * cosine - upper_half * sine_vals, upper_half * cosine + lower_half * sine_vals], axis=-1)

def reference(pool, base_run, gain, w_key, w_value, w_query, src_pos, dst_pos, counts):
    flattened = pool.reshape(SOURCES * SEQ, D)
    widened = flattened.astype(jnp.float32)
    normed = (widened * gain.astype(jnp.float32)[None, :]).astype(jnp.bfloat16)
    squares = lax.optimization_barrier(jnp.sum(widened * widened, axis=1))
    scales = lax.rsqrt(squares / D + epsilon)
    key_all = (scales[:, None] * jnp.dot(normed, w_key, preferred_element_type=jnp.float32)).reshape(SOURCES, SEQ, KV_HEADS * HD)
    value_all = (scales[:, None] * jnp.dot(normed, w_value, preferred_element_type=jnp.float32)).reshape(SOURCES, SEQ, KV_HEADS * HD)
    base_index = base_run[0]
    run_of = jnp.full((CONFIGS, SEQ + 1), base_index, dtype=jnp.int32)
    row_of = jnp.broadcast_to(jnp.arange(SEQ + 1, dtype=jnp.int32)[None, :], (CONFIGS, SEQ + 1))
    in_use = jnp.arange(CAP, dtype=jnp.int32)[None, None, :] < counts[:, :, None]
    targets = jnp.where(in_use, dst_pos, SEQ).astype(jnp.int32)
    config_ids = jnp.broadcast_to(jnp.arange(CONFIGS, dtype=jnp.int32)[:, None, None], targets.shape)
    source_ids = jnp.broadcast_to(jnp.arange(SOURCES, dtype=jnp.int32)[None, :, None], targets.shape)
    run_of = run_of.at[config_ids, targets].set(source_ids)
    row_of = row_of.at[config_ids, targets].set(src_pos.astype(jnp.int32))
    run_of = run_of[:, :SEQ]
    row_of = row_of[:, :SEQ]
    key_raw = key_all[run_of, row_of]
    value_raw = value_all[run_of, row_of]
    positions = jnp.arange(SEQ, dtype=jnp.int32)
    keys = rotate(key_raw.reshape(CONFIGS, SEQ, KV_HEADS, HD), positions).astype(jnp.bfloat16)
    values = value_raw.astype(jnp.bfloat16)
    base_normed = lax.dynamic_index_in_dim(normed.reshape(SOURCES, SEQ, D), base_index, 0, keepdims=False)[SEQ - PROBE:]
    base_scales = lax.dynamic_index_in_dim(scales.reshape(SOURCES, SEQ), base_index, 0, keepdims=False)[SEQ - PROBE:]
    q_raw = base_scales[:, None] * jnp.dot(base_normed, w_query, preferred_element_type=jnp.float32)
    probe_pos = SEQ - PROBE + jnp.arange(PROBE, dtype=jnp.int32)
    queries = rotate(q_raw.reshape(PROBE, Q_HEADS, HD), probe_pos).astype(jnp.bfloat16)
    group_size = Q_HEADS // KV_HEADS
    query_groups = queries.reshape(PROBE, KV_HEADS, group_size, HD).astype(jnp.float32)
    scores = jnp.einsum('pkgh,cskh->cpkgs', query_groups, keys.astype(jnp.float32)) * HD ** (-0.5)
    causal = positions[None, :] <= probe_pos[:, None]
    scores = jnp.where(causal[None, :, None, None, :], scores, -1e+30)
    probs = jax.nn.softmax(scores, axis=-1)
    probs_b = probs.astype(jnp.bfloat16)
    value_heads = values.reshape(CONFIGS, SEQ, KV_HEADS, HD).astype(jnp.float32)
    attended = jnp.einsum('cpkgs,cskh->cpkgh', probs_b.astype(jnp.float32), value_heads)
    attended = attended.astype(jnp.bfloat16).reshape(CONFIGS, PROBE, Q_HEADS * HD)
    return (attended, keys.reshape(CONFIGS, SEQ, KV_HEADS * HD), values)
```

```python
import functools
import math

import jax
import jax.numpy as jnp
import numpy as np
from jax import lax
from jax.experimental import pallas as pl
from jax.experimental.pallas import tpu as pltpu
from jax.sharding import PartitionSpec as P

HD = 128
PROBE = 4
TILE = 16
ROPE_BASE = 500000.0
EPSILON = 1e-05
MESH = pl.DeviceIdType.MESH
f32 = jnp.float32
bf16 = jnp.bfloat16


def rope_tables(first, count):
    half = HD // 2
    freq = np.exp(np.arange(half, dtype=np.float64) * (-2.0 * math.log(ROPE_BASE) / HD))
    angles = np.arange(first, first + count, dtype=np.float64)[:, None] * freq[None, :]
    cosine, sine = np.cos(angles), np.sin(angles)
    return np.stack(
        [np.concatenate([cosine, cosine], 1), np.concatenate([-sine, sine], 1)]
    ).astype(np.float32)


def rotate(rows, cosine, sine):
    return rows * cosine + pltpu.roll(rows, HD // 2, 1) * sine


def lane_groups(squares):
    total = squares[:, :HD]
    for k in range(1, squares.shape[1] // HD):
        total = total + squares[:, k * HD : (k + 1) * HD]
    return total


def gather_kernel(
    n_cfg,
    n_tp,
    pool,
    base,
    gain,
    w_key,
    w_value,
    w_query,
    picks,
    rope,
    arrived,
    base_kv,
    queries,
    rows,
    weights,
    wq,
    masked,
    landed,
    base_rows,
    block,
    part,
    parts,
    chosen,
    kv,
    outgoing,
    acc,
    sums,
    load_sem,
    ring_send,
    ring_recv,
    send,
    recv,
):
    cfg, tp = lax.axis_index("cfg"), lax.axis_index("tp")
    seq, width = rows.shape[1], rows.shape[2]
    half_rows = seq // 2
    model = n_tp * width
    heads = queries.shape[0]
    holders = seq // TILE
    spacing = n_cfg // holders
    is_holder = jnp.logical_and(lax.rem(cfg, spacing) == 0, cfg < holders * spacing)
    my_tile = cfg // spacing
    last_holder = (holders - 1) * spacing
    owner_step = (n_cfg - 1) // (heads - 1)
    is_owner = jnp.logical_and(lax.rem(cfg, owner_step) == 0, cfg < heads * owner_step)
    my_head = cfg // owner_step
    per_plane = n_cfg // n_tp

    loads = [
        pltpu.make_async_copy(pool, rows.at[tp], load_sem.at[0]),
        pltpu.make_async_copy(w_key, weights.at[:, pl.ds(0, HD)], load_sem.at[1]),
        pltpu.make_async_copy(w_value, weights.at[:, pl.ds(HD, HD)], load_sem.at[2]),
        pltpu.make_async_copy(w_query, wq, load_sem.at[3]),
    ]
    for load in loads:
        load.start()

    barrier = pltpu.get_barrier_semaphore()

    @pl.loop(1, n_cfg)
    def _(i):
        pl.semaphore_signal(
            barrier, inc=1, device_id={"cfg": lax.rem(cfg + i, n_cfg)}, device_id_type=MESH
        )

    @pl.loop(1, n_tp)
    def _(i):
        pl.semaphore_signal(
            barrier, inc=1, device_id={"tp": lax.rem(tp + i, n_tp)}, device_id_type=MESH
        )

    loads[0].wait()
    is_base = jnp.full((TILE, width), base[0], jnp.int32) == cfg
    for j in range(holders):
        mine = rows[tp, pl.ds(j * TILE, TILE), :].astype(f32)
        masked[j] = jnp.where(is_base, mine, 0.0).astype(bf16)
    pl.semaphore_wait(barrier, n_cfg - 1 + n_tp - 1)

    def to_cfg(src, dst, which, target):
        return pltpu.make_async_remote_copy(
            src_ref=src,
            dst_ref=dst,
            send_sem=send.at[which],
            recv_sem=recv.at[which],
            device_id={"cfg": target},
            device_id_type=MESH,
        )

    def settle(ref, sem):
        pltpu.make_async_copy(ref, ref, sem).wait()

    def ring(direction, unit):
        hop = unit // 2
        part_no = unit % 2 if direction == 0 else 1 - unit % 2
        sign = 1 if direction == 0 else -1
        slot = lax.rem(tp - sign * hop + n_tp, n_tp)
        piece = rows.at[slot, pl.ds(part_no * half_rows, half_rows)]
        return pltpu.make_async_remote_copy(
            src_ref=piece,
            dst_ref=piece,
            send_sem=ring_send.at[direction, unit],
            recv_sem=ring_recv.at[direction, unit],
            device_id={"tp": lax.rem(tp + sign + n_tp, n_tp)},
            device_id_type=MESH,
        )

    def gains(slot):
        return jnp.concatenate([gain[slot * per_plane + k] for k in range(per_plane)], axis=1)

    def project(slot, part_no):
        piece = pl.ds(part_no * half_rows, half_rows)
        wide = rows[slot, piece, :].astype(f32)
        sums[piece, :] += lane_groups(wide * wide)
        normed = (wide * gains(slot)).astype(bf16)
        depth = pl.ds(pl.multiple_of(slot * width, width), width)
        acc[piece, :] += jnp.dot(normed, weights[depth, :], preferred_element_type=f32)

    units = n_tp - 1

    def ring_step(unit):
        for direction in (0, 1):
            sign = 1 if direction == 0 else -1
            hop = unit // 2 + 1
            part_no = unit % 2 if direction == 0 else 1 - unit % 2
            slot = lax.rem(tp - sign * hop + n_tp, n_tp)
            piece = rows.at[slot, pl.ds(part_no * half_rows, half_rows)]
            pltpu.make_async_copy(piece, piece, ring_recv.at[direction, unit]).wait()
            if unit + 2 < units:
                ring(direction, unit + 2).start()
        for direction in (0, 1):
            sign = 1 if direction == 0 else -1
            hop = unit // 2 + 1
            part_no = unit % 2 if direction == 0 else 1 - unit % 2
            project(lax.rem(tp - sign * hop + n_tp, n_tp), part_no)

    for unit in range(min(2, units)):
        ring(0, unit).start()
        ring(1, unit).start()

    for j in range(holders):

        @pl.when(cfg != j * spacing)
        def _():
            to_cfg(masked.at[j], landed.at[cfg], 0, j * spacing).start()

    @pl.when(is_holder)
    def _():
        landed[cfg] = masked[my_tile]

    acc[...] = jnp.zeros_like(acc)
    sums[...] = jnp.zeros_like(sums)
    for load in loads[1:]:
        load.wait()
    project(tp, 0)
    project(tp, 1)
    column = lax.broadcasted_iota(jnp.int32, (TILE * 4, 2 * seq), 1)

    @pl.loop(0, n_cfg // 4)
    def _(i):
        span = pl.ds(pl.multiple_of(i * TILE * 4, TILE * 4), TILE * 4)
        chosen[span, :] = (column == picks[span, :]).astype(f32).astype(bf16)

    def base_arrives():
        @pl.when(is_holder)
        def _():
            settle(landed.at[pl.ds(0, n_cfg - 1)], recv.at[0])

            def add(s, total):
                return total + landed[s].astype(f32)

            total = lax.fori_loop(0, n_cfg, add, jnp.zeros((TILE, width), f32))
            base_rows[tp] = total.astype(bf16)

            @pl.loop(1, n_tp)
            def _(i):
                pltpu.make_async_remote_copy(
                    src_ref=base_rows.at[tp],
                    dst_ref=base_rows.at[tp],
                    send_sem=send.at[1],
                    recv_sem=recv.at[1],
                    device_id={"tp": lax.rem(tp + i, n_tp)},
                    device_id_type=MESH,
                ).start()

    def base_projects():
        @pl.when(is_holder)
        def _():
            settle(base_rows.at[pl.ds(0, n_tp - 1)], recv.at[1])

            @pl.when(cfg == last_holder)
            def _():
                @pl.loop(1, n_cfg)
                def _(i):
                    target = lax.rem(cfg + i, n_cfg)
                    lanes = pl.ds(pl.multiple_of(lax.rem(target, per_plane) * HD, HD), HD)
                    to_cfg(base_rows.at[target // per_plane, :, lanes], block, 2, target).start()

                lanes = pl.ds(pl.multiple_of(lax.rem(cfg, per_plane) * HD, HD), HD)
                block[...] = base_rows[cfg // per_plane, :, lanes]

            def add(z, state):
                total, squares = state
                wide = base_rows[z].astype(f32)
                normed = (wide * gains(z)).astype(bf16)
                depth = pl.ds(pl.multiple_of(z * width, width), width)
                total += jnp.dot(normed, weights[depth, :], preferred_element_type=f32)
                return total, squares + lane_groups(wide * wide)

            total, squares = lax.fori_loop(
                0, n_tp, add, (jnp.zeros((TILE, 2 * HD), f32), jnp.zeros((TILE, HD), f32))
            )
            scale = lax.rsqrt(jnp.sum(squares, axis=1, keepdims=True) / model + EPSILON)
            base_kv[my_tile] = (total * scale).astype(bf16)

            @pl.loop(1, n_cfg)
            def _(i):
                to_cfg(
                    base_kv.at[my_tile], base_kv.at[my_tile], 3, lax.rem(cfg + i, n_cfg)
                ).start()

    def query_parts():
        @pl.when(cfg != last_holder)
        def _():
            settle(block, recv.at[2])

        wide = block[...].astype(f32)
        normed = (wide * gain[cfg]).astype(bf16)
        total = jnp.dot(normed, wq[...], preferred_element_type=f32)
        squares = wide * wide
        for h in range(heads):
            part[h, pl.ds(0, 8), :] = total[8:, h * HD : (h + 1) * HD]
            part[h, pl.ds(8, 8), :] = squares[8:, :]
        for h in range(heads):

            @pl.when(cfg != h * owner_step)
            def _():
                to_cfg(part.at[h], parts.at[cfg], 4, h * owner_step).start()

        @pl.when(is_owner)
        def _():
            parts[cfg] = part[my_head]

    def query_sums():
        @pl.when(is_owner)
        def _():
            settle(parts.at[pl.ds(0, n_cfg - 1)], recv.at[4])

            def add(s, total):
                return total + parts[s]

            total = lax.fori_loop(0, n_cfg, add, jnp.zeros((TILE, HD), f32))
            scale = lax.rsqrt(jnp.sum(total[8:], axis=1, keepdims=True) / model + EPSILON)
            queries[my_head] = rotate(total[:8] * scale, rope[0], rope[1])

            @pl.loop(1, n_cfg)
            def _(i):
                to_cfg(
                    queries.at[my_head], queries.at[my_head], 5, lax.rem(cfg + i, n_cfg)
                ).start()

    beside = {1: base_arrives, 2: base_projects, 3: query_parts, 4: query_sums}
    for unit in range(units):
        ring_step(unit)
        if unit in beside:
            beside.pop(unit)()
    for unit in sorted(beside):
        beside[unit]()

    scale = lax.rsqrt(jnp.sum(sums[...], axis=1, keepdims=True) / model + EPSILON)
    scaled = (acc[...] * scale).astype(bf16)
    kv[pl.ds(0, seq), :] = scaled[:, :HD]
    kv[pl.ds(seq, seq), :] = scaled[:, HD:]
    picked = jnp.dot(chosen[...], kv[...], preferred_element_type=f32).astype(bf16)
    outgoing[...] = picked.reshape(n_cfg, TILE, HD)

    @pl.loop(1, n_cfg)
    def _(i):
        target = lax.rem(cfg + i, n_cfg)
        to_cfg(outgoing.at[target], arrived.at[cfg], 6, target).start()

    arrived[cfg] = outgoing[cfg]

    for unit in range(units):
        for direction in (0, 1):
            ring(direction, unit).wait_send()

    def both(condition, if_true, if_false):
        pl.when(condition)(if_true)
        pl.when(jnp.logical_not(condition))(if_false)

    both(
        is_holder,
        lambda: settle(masked.at[pl.ds(0, holders - 1)], send.at[0]),
        lambda: settle(masked, send.at[0]),
    )

    @pl.when(is_holder)
    def _():
        settle(base_rows.at[pl.ds(0, n_tp - 1)], send.at[1])
        settle(landed.at[pl.ds(0, n_cfg - 1), :, pl.ds(0, 2 * HD)], send.at[3])

    @pl.when(cfg == last_holder)
    def _():
        settle(arrived.at[pl.ds(0, n_cfg - 1)], send.at[2])

    both(
        is_owner,
        lambda: settle(part.at[pl.ds(0, heads - 1)], send.at[4]),
        lambda: settle(part, send.at[4]),
    )
    both(
        is_holder,
        lambda: settle(base_kv.at[pl.ds(0, holders - 1)], recv.at[3]),
        lambda: settle(base_kv, recv.at[3]),
    )
    both(
        is_owner,
        lambda: settle(queries.at[pl.ds(0, heads - 1)], recv.at[5]),
        lambda: settle(queries, recv.at[5]),
    )

    @pl.when(is_owner)
    def _():
        settle(arrived.at[pl.ds(0, n_cfg - 1)], send.at[5])

    settle(outgoing.at[pl.ds(0, n_cfg - 1)], send.at[6])
    settle(arrived.at[pl.ds(0, n_cfg - 1)], recv.at[6])


def attend_kernel(arrived, base_kv, queries, targets, rope, attended, keys, values):
    n_configs, seq = keys.shape[0], keys.shape[1]
    heads = queries.shape[0]
    spliced = arrived[...].astype(f32)
    slots = spliced.shape[0] * 8
    rows = jnp.concatenate(
        [spliced[:, :8, :].reshape(slots, HD), spliced[:, 8:, :].reshape(slots, HD)], axis=1
    ).astype(bf16)
    base = base_kv[...].reshape(seq, 2 * HD).astype(f32)
    probes = queries[...].reshape(heads * 8, HD).astype(bf16)
    position = lax.broadcasted_iota(jnp.int32, (seq, slots), 0)
    probe_row = lax.broadcasted_iota(jnp.int32, (heads * 8, seq), 0)
    causal = lax.broadcasted_iota(jnp.int32, (heads * 8, seq), 1) <= seq - 8 + lax.rem(probe_row, 8)
    cosine, sine = rope[0], rope[1]
    for i in range(n_configs):
        onehot = (position == targets[pl.ds(i, 1), :]).astype(f32)
        covered = jnp.max(onehot, axis=1, keepdims=True)
        taken = jnp.dot(onehot.astype(bf16), rows, preferred_element_type=f32)
        both = jnp.where(covered > 0.0, taken, base)
        key = rotate(both[:, :HD], cosine, sine).astype(bf16)
        value = both[:, HD:].astype(bf16)
        keys[i] = key
        values[i] = value
        scores = lax.dot_general(
            probes, key, (((1,), (1,)), ((), ())), preferred_element_type=f32
        ) * HD ** (-0.5)
        scores = jnp.where(causal, scores, -1e30)
        top = jnp.max(scores, axis=1, keepdims=True)
        grown = jnp.exp(scores - top)
        probs = (grown / jnp.sum(grown, axis=1, keepdims=True)).astype(bf16)
        out = jnp.dot(probs, value, preferred_element_type=f32)
        for h in range(heads):
            attended[i, :, h * HD : (h + 1) * HD] = out[h * 8 + 8 - PROBE : h * 8 + 8, :].astype(bf16)


def body(n_cfg, n_tp, pool, base_run, gain, w_key, w_value, w_query, src_pos, dst_pos, counts):
    seq, width = pool.shape[1], pool.shape[2]
    n_configs, cap = dst_pos.shape[0], dst_pos.shape[2]
    used = n_configs * cap
    heads = w_query.shape[1] // HD
    holders = seq // TILE
    gains = gain.astype(f32).reshape(n_cfg, 1, HD)
    wanted = src_pos.reshape(n_cfg, used)
    wanted = jnp.pad(wanted, ((0, 0), (0, 8 - used)), constant_values=-2 * seq)
    picks = jnp.concatenate([wanted, wanted + seq], axis=1).reshape(n_cfg * TILE, 1)
    in_use = jnp.arange(cap, dtype=jnp.int32)[None, None, :] < counts[:, :, None]
    target = jnp.where(in_use, dst_pos, -1)[:, :, None, :]
    own = jnp.arange(n_configs)[:, None] == jnp.arange(n_configs)[None, :]
    target = jnp.where(own[:, None, :, None], target, -1).reshape(n_configs, n_cfg, used)
    targets = jnp.pad(target, ((0, 0), (0, 0), (0, 8 - used)), constant_values=-1)
    targets = targets.reshape(n_configs, n_cfg * 8)
    vmem, anywhere = pl.BlockSpec(memory_space=pltpu.VMEM), pl.BlockSpec(memory_space=pl.ANY)
    smem = pl.BlockSpec(memory_space=pltpu.SMEM)
    dma, hops = pltpu.SemaphoreType.DMA, n_tp - 1
    arrived, base_kv, queries = pl.pallas_call(
        functools.partial(gather_kernel, n_cfg, n_tp),
        out_shape=(
            jax.ShapeDtypeStruct((n_cfg, TILE, HD), bf16),
            jax.ShapeDtypeStruct((holders, TILE, 2 * HD), bf16),
            jax.ShapeDtypeStruct((heads, 8, HD), f32),
        ),
        in_specs=[anywhere, smem, vmem, anywhere, anywhere, anywhere, vmem, vmem],
        out_specs=(vmem, vmem, vmem),
        scratch_shapes=[
            pltpu.VMEM((n_tp, seq, width), bf16),
            pltpu.VMEM((n_tp * width, 2 * HD), bf16),
            pltpu.VMEM(w_query.shape, bf16),
            pltpu.VMEM((holders, TILE, width), bf16),
            pltpu.VMEM((n_cfg, TILE, width), bf16),
            pltpu.VMEM((n_tp, TILE, width), bf16),
            pltpu.VMEM((TILE, HD), bf16),
            pltpu.VMEM((heads, TILE, HD), f32),
            pltpu.VMEM((n_cfg, TILE, HD), f32),
            pltpu.VMEM((n_cfg * TILE, 2 * seq), bf16),
            pltpu.VMEM((2 * seq, HD), bf16),
            pltpu.VMEM((n_cfg, TILE, HD), bf16),
            pltpu.VMEM((seq, 2 * HD), f32),
            pltpu.VMEM((seq, HD), f32),
            dma((4,)),
            dma((2, hops)),
            dma((2, hops)),
            dma((7,)),
            dma((7,)),
        ],
        compiler_params=pltpu.CompilerParams(
            collective_id=0, has_side_effects=True, vmem_limit_bytes=40 << 20
        ),
    )(
        pool[0],
        base_run,
        gains,
        w_key,
        w_value,
        w_query,
        picks,
        jnp.asarray(rope_tables(seq - 8, 8)),
    )
    return pl.pallas_call(
        attend_kernel,
        out_shape=(
            jax.ShapeDtypeStruct((n_configs, PROBE, heads * HD), bf16),
            jax.ShapeDtypeStruct((n_configs, seq, HD), bf16),
            jax.ShapeDtypeStruct((n_configs, seq, HD), bf16),
        ),
        in_specs=[vmem] * 5,
        out_specs=(vmem, vmem, vmem),
        compiler_params=pltpu.CompilerParams(vmem_limit_bytes=40 << 20),
    )(arrived, base_kv, queries, targets, jnp.asarray(rope_tables(0, seq)))


def solution(mesh):
    placed = (
        P("cfg", None, "tp"),
        P(),
        P(),
        P(None, "tp"),
        P(None, "tp"),
        P("cfg", "tp"),
        P(None, "cfg", None),
        P("cfg", None, None),
        P("cfg", None),
    )
    return jax.shard_map(
        functools.partial(body, mesh.shape["cfg"], mesh.shape["tp"]),
        mesh=mesh,
        in_specs=placed,
        out_specs=(P("cfg", None, "tp"), P("cfg", None, "tp"), P("cfg", None, "tp")),
        check_vma=False,
    )
```

```python
import functools
import math

import jax
import jax.numpy as jnp
import numpy as np
from jax import lax
from jax.experimental import pallas as pl
from jax.experimental.pallas import tpu as pltpu
from jax.sharding import PartitionSpec as P

HD = 128
PROBE = 4
TILE = 16
ROPE_BASE = 500000.0
EPSILON = 1e-05
MESH = pl.DeviceIdType.MESH
f32 = jnp.float32
bf16 = jnp.bfloat16


def rope_tables(first, count):
    half = HD // 2
    freq = np.exp(np.arange(half, dtype=np.float64) * (-2.0 * math.log(ROPE_BASE) / HD))
    angles = np.arange(first, first + count, dtype=np.float64)[:, None] * freq[None, :]
    cosine, sine = np.cos(angles), np.sin(angles)
    return np.stack(
        [np.concatenate([cosine, cosine], 1), np.concatenate([-sine, sine], 1)]
    ).astype(np.float32)


def rotate(rows, cosine, sine):
    return rows * cosine + pltpu.roll(rows, HD // 2, 1) * sine


def lane_groups(squares):
    total = squares[:, :HD]
    for k in range(1, squares.shape[1] // HD):
        total = total + squares[:, k * HD : (k + 1) * HD]
    return total


def sweep_kernel(
    n_cfg,
    n_tp,
    pool,
    base,
    gain,
    w_key,
    w_value,
    w_query,
    src_pos,
    dst_pos,
    counts,
    rope_table,
    attended,
    keys,
    values,
    rows,
    weights,
    wq,
    gain_raw,
    gain_wide,
    src,
    dst,
    used,
    rope,
    masked,
    row_sums,
    middle,
    landed,
    base_rows,
    block,
    part,
    parts,
    queries,
    base_kv,
    chosen,
    placed,
    uncovered,
    kv,
    outgoing,
    arrived,
    acc,
    sums,
    many,
    load_sem,
    ring_send,
    ring_recv,
    send,
    recv,
):
    cfg, tp = lax.axis_index("cfg"), lax.axis_index("tp")
    seq, width = rows.shape[1], rows.shape[2]
    half_rows = seq // 2
    model = n_tp * width
    heads = queries.shape[0]
    group, tile = masked.shape[0], masked.shape[1]
    rings = n_cfg // group
    place, turn = lax.rem(cfg, group), cfg // group
    holder = lax.rem(place, rings) * group + place
    is_holder = cfg == holder
    last_holder = (group - 1) % rings * group + group - 1
    owner_step = (n_cfg - 1) // (heads - 1)
    is_owner = jnp.logical_and(lax.rem(cfg, owner_step) == 0, cfg < heads * owner_step)
    my_head = cfg // owner_step
    per_plane = n_cfg // n_tp

    loads = [
        pltpu.make_async_copy(source, target, load_sem.at[i])
        for i, (source, target) in enumerate(
            (
                (pool, rows.at[tp]),
                (gain, gain_raw),
                (w_key, weights.at[:, pl.ds(0, HD)]),
                (w_value, weights.at[:, pl.ds(HD, HD)]),
                (w_query, wq),
                (src_pos, src),
                (dst_pos, dst),
                (counts, used),
                (rope_table, rope),
            )
        )
    ]
    for load in loads:
        load.start()

    barrier = pltpu.get_barrier_semaphore()

    @pl.loop(1, n_cfg)
    def _(i):
        pl.semaphore_signal(
            barrier, inc=1, device_id={"cfg": lax.rem(cfg + i, n_cfg)}, device_id_type=MESH
        )

    @pl.loop(1, n_tp)
    def _(i):
        pl.semaphore_signal(
            barrier, inc=1, device_id={"tp": lax.rem(tp + i, n_tp)}, device_id_type=MESH
        )

    loads[0].wait()
    is_base = jnp.full((tile, width), base[0], jnp.int32) == cfg
    for j in range(group):
        mine = rows[tp, pl.ds(j * tile, tile), :].astype(f32)
        masked[j] = jnp.where(is_base, mine, 0.0).astype(bf16)
    pl.semaphore_wait(barrier, n_cfg - 1 + n_tp - 1)

    def to_cfg(src, dst, which, target):
        return pltpu.make_async_remote_copy(
            src_ref=src,
            dst_ref=dst,
            send_sem=send.at[which],
            recv_sem=recv.at[which],
            device_id={"cfg": target},
            device_id_type=MESH,
        )

    def settle(ref, sem):
        pltpu.make_async_copy(ref, ref, sem).wait()

    def ring(direction, unit):
        hop = unit // 2
        part_no = unit % 2 if direction == 0 else 1 - unit % 2
        sign = 1 if direction == 0 else -1
        slot = lax.rem(tp - sign * hop + n_tp, n_tp)
        piece = rows.at[slot, pl.ds(part_no * half_rows, half_rows)]
        return pltpu.make_async_remote_copy(
            src_ref=piece,
            dst_ref=piece,
            send_sem=ring_send.at[direction, unit],
            recv_sem=ring_recv.at[direction, unit],
            device_id={"tp": lax.rem(tp + sign + n_tp, n_tp)},
            device_id_type=MESH,
        )

    def gains(slot):
        eight = gain_wide[slot]
        return jnp.concatenate([eight[k : k + 1, :] for k in range(per_plane)], axis=1)

    def project(slot, part_no):
        piece = pl.ds(part_no * half_rows, half_rows)
        wide = rows[slot, piece, :].astype(f32)
        sums[piece, :] += lane_groups(wide * wide)
        normed = (wide * gains(slot)).astype(bf16)
        depth = pl.ds(pl.multiple_of(slot * width, width), width)
        acc[piece, :] += jnp.dot(normed, weights[depth, :], preferred_element_type=f32)

    units = n_tp - 1

    def ring_step(unit):
        for direction in (0, 1):
            sign = 1 if direction == 0 else -1
            hop = unit // 2 + 1
            part_no = unit % 2 if direction == 0 else 1 - unit % 2
            slot = lax.rem(tp - sign * hop + n_tp, n_tp)
            piece = rows.at[slot, pl.ds(part_no * half_rows, half_rows)]
            pltpu.make_async_copy(piece, piece, ring_recv.at[direction, unit]).wait()
            if unit + 2 < units:
                ring(direction, unit + 2).start()
        for direction in (0, 1):
            sign = 1 if direction == 0 else -1
            hop = unit // 2 + 1
            part_no = unit % 2 if direction == 0 else 1 - unit % 2
            project(lax.rem(tp - sign * hop + n_tp, n_tp), part_no)

    for unit in range(min(2, units)):
        ring(0, unit).start()
        ring(1, unit).start()

    @pl.loop(1, group)
    def _(i):
        other = lax.rem(place + i, group)
        to_cfg(masked.at[other], row_sums.at[place], 0, turn * group + other).start()

    row_sums[place] = masked[place]
    acc[...] = jnp.zeros_like(acc)
    sums[...] = jnp.zeros_like(sums)
    kv[...] = jnp.zeros_like(kv)
    for load in loads[1:]:
        load.wait()
    for z in range(n_tp):
        gain_wide[z] = gain_raw[...].astype(f32)[z * per_plane : (z + 1) * per_plane, :]
    project(tp, 0)
    project(tp, 1)

    def base_meets():
        settle(row_sums.at[pl.ds(0, group - 1)], recv.at[0])
        total = row_sums[0].astype(f32)
        for q in range(1, group):
            total += row_sums[q].astype(f32)
        middle[...] = total.astype(bf16)

        @pl.when(jnp.logical_not(is_holder))
        def _():
            to_cfg(middle, landed.at[turn], 7, holder).start()

        @pl.when(is_holder)
        def _():
            landed[turn] = middle[...]

    padded = kv.shape[0] // 2
    span_rows = TILE * 4
    config = lax.broadcasted_iota(jnp.int32, (span_rows, src.shape[1]), 1)
    row_no = lax.broadcasted_iota(jnp.int32, (padded, src.shape[1]), 0)
    cap = src.shape[0]
    n_configs = keys.shape[0]
    asked = [(row_no == src[j : j + 1, :]).astype(f32).astype(bf16) for j in range(cap)]
    is_key = lax.broadcasted_iota(jnp.int32, (span_rows, padded), 0) % TILE < 8

    @pl.loop(0, n_cfg // 4)
    def _(i):
        span = pl.ds(pl.multiple_of(i * span_rows, span_rows), span_rows)
        slot = lax.broadcasted_iota(jnp.int32, (span_rows, src.shape[1]), 0)
        target = i * 4 + lax.shift_right_logical(slot, 4)
        slot = slot & 7
        found = jnp.zeros((span_rows, padded), f32)
        for j in range(cap):
            wanted = jnp.zeros(slot.shape, f32)
            for k in range(n_configs):
                hit = jnp.logical_and(config == target * n_configs + k, slot == k * cap + j)
                wanted = wanted + hit.astype(f32)
            found += lax.dot_general(
                wanted.astype(bf16),
                asked[j],
                (((1,), (1,)), ((), ())),
                preferred_element_type=f32,
            )
        chosen[span, pl.ds(0, padded)] = jnp.where(is_key, found, 0.0).astype(bf16)
        chosen[span, pl.ds(padded, padded)] = jnp.where(is_key, 0.0, found).astype(bf16)

    slots = n_cfg * 8
    source = lax.broadcasted_iota(jnp.int32, (n_cfg, slots), 0)
    slot = lax.broadcasted_iota(jnp.int32, (n_cfg, slots), 1)
    spread = (source == lax.shift_right_logical(slot, 3)).astype(f32).astype(bf16)
    position = lax.broadcasted_iota(jnp.int32, (seq, slots), 0).astype(f32) + 1.0
    slot_of = lax.broadcasted_iota(jnp.int32, (8, slots), 1) & 7
    order = lax.broadcasted_iota(jnp.int32, (cap, n_cfg), 0)
    for i in range(n_configs):
        valid = order < used[i : i + 1, :]
        goal = jnp.where(valid, dst[i] + 1, 0).astype(f32)
        goal = jnp.concatenate([goal, jnp.zeros((8 - cap, n_cfg), f32)], axis=0)
        wide = jnp.dot(goal.astype(bf16), spread, preferred_element_type=f32)
        row_id = lax.broadcasted_iota(jnp.int32, (8, slots), 0)
        mine = jnp.logical_and(slot_of == row_id + i * cap, row_id < cap)
        goal = jnp.sum(jnp.where(mine, wide, 0.0), axis=0, keepdims=True)
        onehot = (position == goal).astype(f32)
        placed[pl.ds(i * seq, seq), :] = onehot.astype(bf16)
        free = 1.0 - jnp.max(onehot, axis=1, keepdims=True)
        uncovered[pl.ds(i * seq, seq), :] = jnp.broadcast_to(free, (seq, 2 * HD))

    def base_arrives():
        @pl.when(is_holder)
        def _():
            settle(landed.at[pl.ds(0, rings - 1)], recv.at[7])
            total = landed[0].astype(f32)
            for y in range(1, rings):
                total += landed[y].astype(f32)
            base_rows[tp] = total.astype(bf16)

            @pl.loop(1, n_tp)
            def _(i):
                pltpu.make_async_remote_copy(
                    src_ref=base_rows.at[tp],
                    dst_ref=base_rows.at[tp],
                    send_sem=send.at[1],
                    recv_sem=recv.at[1],
                    device_id={"tp": lax.rem(tp + i, n_tp)},
                    device_id_type=MESH,
                ).start()

    def base_projects():
        @pl.when(is_holder)
        def _():
            settle(base_rows.at[pl.ds(0, n_tp - 1)], recv.at[1])

            @pl.when(cfg == last_holder)
            def _():
                @pl.loop(1, n_cfg)
                def _(i):
                    target = lax.rem(cfg + i, n_cfg)
                    lanes = pl.ds(pl.multiple_of(lax.rem(target, per_plane) * HD, HD), HD)
                    to_cfg(base_rows.at[target // per_plane, :, lanes], block, 2, target).start()

                lanes = pl.ds(pl.multiple_of(lax.rem(cfg, per_plane) * HD, HD), HD)
                block[...] = base_rows[cfg // per_plane, :, lanes]

            def add(z, state):
                total, squares = state
                wide = base_rows[z].astype(f32)
                normed = (wide * gains(z)).astype(bf16)
                depth = pl.ds(pl.multiple_of(z * width, width), width)
                total += jnp.dot(normed, weights[depth, :], preferred_element_type=f32)
                return total, squares + lane_groups(wide * wide)

            total, squares = lax.fori_loop(
                0, n_tp, add, (jnp.zeros((tile, 2 * HD), f32), jnp.zeros((tile, HD), f32))
            )
            scale = lax.rsqrt(jnp.sum(squares, axis=1, keepdims=True) / model + EPSILON)
            base_kv[place] = (total * scale).astype(bf16)

            @pl.loop(1, n_cfg)
            def _(i):
                to_cfg(
                    base_kv.at[place], base_kv.at[place], 3, lax.rem(cfg + i, n_cfg)
                ).start()

    def query_parts():
        @pl.when(cfg != last_holder)
        def _():
            settle(block, recv.at[2])

        wide = block[...].astype(f32)[tile - 8 :, :]
        own_gain = gain_wide[cfg // per_plane]
        pick = lax.broadcasted_iota(jnp.int32, own_gain.shape, 0) == lax.rem(cfg, per_plane)
        own_gain = jnp.sum(jnp.where(pick, own_gain, 0.0), axis=0, keepdims=True)
        normed = (wide * own_gain).astype(bf16)
        total = jnp.dot(normed, wq[...], preferred_element_type=f32)
        squares = wide * wide
        for h in range(heads):
            part[h, pl.ds(0, 8), :] = total[:, h * HD : (h + 1) * HD]
            part[h, pl.ds(8, 8), :] = squares
        for h in range(heads):

            @pl.when(cfg != h * owner_step)
            def _():
                to_cfg(part.at[h], parts.at[cfg], 4, h * owner_step).start()

        @pl.when(is_owner)
        def _():
            parts[cfg] = part[my_head]

    def query_sums():
        @pl.when(is_owner)
        def _():
            settle(parts.at[pl.ds(0, n_cfg - 1)], recv.at[4])

            def add(s, total):
                return total + parts[s]

            total = lax.fori_loop(0, n_cfg, add, jnp.zeros((TILE, HD), f32))
            scale = lax.rsqrt(jnp.sum(total[8:], axis=1, keepdims=True) / model + EPSILON)
            queries[my_head] = rotate(
                total[:8] * scale, rope[0, pl.ds(seq - 8, 8), :], rope[1, pl.ds(seq - 8, 8), :]
            )

            @pl.loop(1, n_cfg)
            def _(i):
                to_cfg(
                    queries.at[my_head], queries.at[my_head], 5, lax.rem(cfg + i, n_cfg)
                ).start()

    beside = {0: base_meets, 1: base_arrives, 2: base_projects, 3: query_parts, 4: query_sums}
    for unit in range(units):
        ring_step(unit)
        if unit in beside:
            beside.pop(unit)()
    for unit in sorted(beside):
        beside[unit]()

    scale = lax.rsqrt(jnp.sum(sums[...], axis=1, keepdims=True) / model + EPSILON)
    scaled = (acc[...] * scale).astype(bf16)
    kv[pl.ds(0, seq), :] = scaled[:, :HD]
    kv[pl.ds(padded, seq), :] = scaled[:, HD:]
    picked = jnp.dot(chosen[...], kv[...], preferred_element_type=f32).astype(bf16)
    outgoing[...] = picked.reshape(n_cfg, TILE, HD)

    @pl.loop(1, n_cfg)
    def _(i):
        target = lax.rem(cfg + i, n_cfg)
        to_cfg(outgoing.at[target], arrived.at[cfg], 6, target).start()

    arrived[cfg] = outgoing[cfg]

    def both(condition, if_true, if_false):
        pl.when(condition)(if_true)
        pl.when(jnp.logical_not(condition))(if_false)

    for unit in range(units):
        for direction in (0, 1):
            ring(direction, unit).wait_send()
    settle(masked.at[pl.ds(0, group - 1)], send.at[0])

    @pl.when(jnp.logical_not(is_holder))
    def _():
        settle(middle, send.at[7])

    @pl.when(is_holder)
    def _():
        settle(base_rows.at[pl.ds(0, n_tp - 1)], send.at[1])
        settle(many.at[pl.ds(0, n_cfg - 1), :, pl.ds(0, 2 * HD)], send.at[3])

    @pl.when(cfg == last_holder)
    def _():
        settle(many.at[pl.ds(0, n_cfg - 1), :, pl.ds(0, HD)], send.at[2])

    both(
        is_owner,
        lambda: settle(part.at[pl.ds(0, heads - 1)], send.at[4]),
        lambda: settle(part, send.at[4]),
    )
    both(
        is_holder,
        lambda: settle(base_kv.at[pl.ds(0, group - 1)], recv.at[3]),
        lambda: settle(base_kv, recv.at[3]),
    )
    both(
        is_owner,
        lambda: settle(queries.at[pl.ds(0, heads - 1)], recv.at[5]),
        lambda: settle(queries, recv.at[5]),
    )

    @pl.when(is_owner)
    def _():
        settle(arrived.at[pl.ds(0, n_cfg - 1)], send.at[5])

    settle(outgoing.at[pl.ds(0, n_cfg - 1)], send.at[6])
    base_all = base_kv[...].astype(f32).reshape(seq, 2 * HD)
    probes = queries[...].reshape(heads * 8, HD).astype(bf16)
    probe_row = lax.broadcasted_iota(jnp.int32, (heads * 8, seq), 0) & 7
    causal = lax.broadcasted_iota(jnp.int32, (heads * 8, seq), 1) <= seq - 8 + probe_row
    settle(arrived.at[pl.ds(0, n_cfg - 1)], recv.at[6])

    spliced = arrived[...].astype(f32)
    taken_rows = jnp.concatenate(
        [spliced[:, :8, :].reshape(slots, HD), spliced[:, 8:, :].reshape(slots, HD)], axis=1
    ).astype(bf16)
    for i in range(n_configs):
        span = pl.ds(i * seq, seq)
        taken = jnp.dot(placed[span, :], taken_rows, preferred_element_type=f32)
        mixed = jnp.where(uncovered[span, :] > 0.5, base_all, taken)
        key = rotate(mixed[:, :HD], rope[0], rope[1]).astype(bf16)
        value = mixed[:, HD:].astype(bf16)
        keys[i] = key
        values[i] = value
        scores = lax.dot_general(
            probes, key, (((1,), (1,)), ((), ())), preferred_element_type=f32
        ) * HD ** (-0.5)
        scores = jnp.where(causal, scores, -1e30)
        top = jnp.max(scores, axis=1, keepdims=True)
        grown = jnp.exp(scores - top)
        probs = (grown / jnp.sum(grown, axis=1, keepdims=True)).astype(bf16)
        out = jnp.dot(probs, value, preferred_element_type=f32)
        for h in range(heads):
            attended[i, :, h * HD : (h + 1) * HD] = out[h * 8 + 8 - PROBE : h * 8 + 8, :].astype(bf16)


def body(n_cfg, n_tp, pool, base_run, gain, w_key, w_value, w_query, src_pos, dst_pos, counts):
    seq, width = pool.shape[1], pool.shape[2]
    n_configs, cap = dst_pos.shape[0], dst_pos.shape[2]
    heads = w_query.shape[1] // HD
    group = 1 << (n_cfg.bit_length() // 2)
    tile = seq // group
    padded = -(-seq // HD) * HD
    vmem, anywhere = pl.BlockSpec(memory_space=pltpu.VMEM), pl.BlockSpec(memory_space=pl.ANY)
    smem = pl.BlockSpec(memory_space=pltpu.SMEM)
    dma, hops = pltpu.SemaphoreType.DMA, n_tp - 1
    return pl.pallas_call(
        functools.partial(sweep_kernel, n_cfg, n_tp),
        out_shape=(
            jax.ShapeDtypeStruct((n_configs, PROBE, heads * HD), bf16),
            jax.ShapeDtypeStruct((n_configs, seq, HD), bf16),
            jax.ShapeDtypeStruct((n_configs, seq, HD), bf16),
        ),
        in_specs=[anywhere, smem] + [anywhere] * 8,
        out_specs=(vmem, vmem, vmem),
        scratch_shapes=[
            pltpu.VMEM((n_tp, seq, width), bf16),
            pltpu.VMEM((n_tp * width, 2 * HD), bf16),
            pltpu.VMEM(w_query.shape, bf16),
            pltpu.VMEM((n_cfg, HD), bf16),
            pltpu.VMEM((n_tp, n_cfg // n_tp, HD), f32),
            pltpu.VMEM((cap, n_configs * n_cfg), jnp.int32),
            pltpu.VMEM((n_configs, cap, n_cfg), jnp.int32),
            pltpu.VMEM((n_configs, n_cfg), jnp.int32),
            pltpu.VMEM((2, seq, HD), f32),
            pltpu.VMEM((group, tile, width), bf16),
            pltpu.VMEM((group, tile, width), bf16),
            pltpu.VMEM((tile, width), bf16),
            pltpu.VMEM((n_cfg // group, tile, width), bf16),
            pltpu.VMEM((n_tp, tile, width), bf16),
            pltpu.VMEM((tile, HD), bf16),
            pltpu.VMEM((heads, TILE, HD), f32),
            pltpu.VMEM((n_cfg, TILE, HD), f32),
            pltpu.VMEM((heads, 8, HD), f32),
            pltpu.VMEM((group, tile, 2 * HD), bf16),
            pltpu.VMEM((n_cfg * TILE, 2 * padded), bf16),
            pltpu.VMEM((n_configs * seq, n_cfg * 8), bf16),
            pltpu.VMEM((n_configs * seq, 2 * HD), f32),
            pltpu.VMEM((2 * padded, HD), bf16),
            pltpu.VMEM((n_cfg, TILE, HD), bf16),
            pltpu.VMEM((n_cfg, TILE, HD), bf16),
            pltpu.VMEM((seq, 2 * HD), f32),
            pltpu.VMEM((seq, HD), f32),
            pltpu.VMEM((n_cfg, tile, 2 * HD), bf16),
            dma((9,)),
            dma((2, hops)),
            dma((2, hops)),
            dma((8,)),
            dma((8,)),
        ],
        compiler_params=pltpu.CompilerParams(
            collective_id=0, has_side_effects=True, vmem_limit_bytes=60 << 20
        ),
    )(
        pool[0],
        base_run,
        gain.reshape(n_cfg, HD),
        w_key,
        w_value,
        w_query,
        jnp.transpose(src_pos[:, 0, :], (1, 0)),
        jnp.transpose(dst_pos, (0, 2, 1)),
        counts,
        jnp.asarray(rope_tables(0, seq)),
    )


def solution(mesh):
    placed = (
        P("cfg", None, "tp"),
        P(),
        P(),
        P(None, "tp"),
        P(None, "tp"),
        P("cfg", "tp"),
        P(None, "cfg", None),
        P("cfg", None, None),
        P("cfg", None),
    )
    return jax.shard_map(
        functools.partial(body, mesh.shape["cfg"], mesh.shape["tp"]),
        mesh=mesh,
        in_specs=placed,
        out_specs=(P("cfg", None, "tp"), P("cfg", None, "tp"), P("cfg", None, "tp")),
        check_vma=False,
    )
```

```python
import functools
import math

import jax
import jax.numpy as jnp
import numpy as np
from jax import lax
from jax.experimental import pallas as pl
from jax.experimental.pallas import tpu as pltpu
from jax.sharding import PartitionSpec as P

HD = 128
PROBE = 4
TILE = 16
ROPE_BASE = 500000.0
EPSILON = 1e-05
MESH = pl.DeviceIdType.MESH
f32 = jnp.float32
bf16 = jnp.bfloat16


def rope_tables(first, count):
    half = HD // 2
    freq = np.exp(np.arange(half, dtype=np.float64) * (-2.0 * math.log(ROPE_BASE) / HD))
    angles = np.arange(first, first + count, dtype=np.float64)[:, None] * freq[None, :]
    cosine, sine = np.cos(angles), np.sin(angles)
    return np.stack(
        [np.concatenate([cosine, cosine], 1), np.concatenate([-sine, sine], 1)]
    ).astype(np.float32)


def rotate(rows, cosine, sine):
    return rows * cosine + pltpu.roll(rows, HD // 2, 1) * sine


def lane_groups(squares):
    total = squares[:, :HD]
    for k in range(1, squares.shape[1] // HD):
        total = total + squares[:, k * HD : (k + 1) * HD]
    return total


def sweep_kernel(
    n_cfg,
    n_tp,
    pool,
    base_run,
    gain,
    w_key,
    w_value,
    w_query,
    src_pos,
    rope_table,
    dst_pos,
    counts,
    arrived,
    base_kv,
    queries,
    splices,
    base,
    rows,
    weights,
    wq,
    gain_raw,
    gain_wide,
    src,
    dst,
    used,
    rope,
    placed,
    masked,
    row_sums,
    middle,
    landed,
    base_rows,
    probe,
    probes_met,
    block,
    part,
    parts,
    my_queries,
    my_base_kv,
    chosen,
    kv,
    outgoing,
    acc,
    sums,
    load_sem,
    ring_send,
    ring_recv,
    send,
    recv,
):
    cfg, tp = lax.axis_index("cfg"), lax.axis_index("tp")
    seq, width = rows.shape[1], rows.shape[2]
    half_rows = seq // 2
    model = n_tp * width
    heads = queries.shape[0]
    group, tile = masked.shape[0], masked.shape[1]
    rings = n_cfg // group
    place, turn = lax.rem(cfg, group), cfg // group
    holder = lax.rem(place, rings) * group + place
    is_holder = cfg == holder

    def owner(head):
        return (head + rings // 2) % rings * group + head

    is_owner = jnp.logical_and(turn == lax.rem(place + rings // 2, rings), place < heads)
    my_head = lax.rem(place, heads)
    per_plane = n_cfg // n_tp
    makes_block = cfg // per_plane == tp

    loads = [
        pltpu.make_async_copy(source, target, load_sem.at[i])
        for i, (source, target) in enumerate(
            (
                (pool, rows.at[tp]),
                (base_run, base),
                (gain, gain_raw),
                (w_key, weights.at[:, pl.ds(0, HD)]),
                (w_value, weights.at[:, pl.ds(HD, HD)]),
                (w_query, wq),
                (src_pos, src),
                (rope_table, rope),
                (dst_pos, dst),
                (counts, used),
            )
        )
    ]
    for load in loads:
        load.start()

    def outward(i, size):
        step = lax.div(i + 1, 2)
        return lax.rem(size // 2 + jnp.where(lax.rem(i, 2) == 0, step, size - step), size)

    def peer(i):
        across = lax.rem(i, group)
        y = lax.rem(turn + outward(lax.div(i, group), rings), rings)
        x = lax.rem(lax.div(place, 2) + outward(lax.div(across, 2), group // 2), group // 2)
        core = lax.rem(place + 1 - lax.rem(across, 2), 2)
        return y * group + x * 2 + core

    barrier = pltpu.get_barrier_semaphore()

    @pl.loop(0, n_cfg - 1)
    def _(i):
        pl.semaphore_signal(barrier, inc=1, device_id={"cfg": peer(i)}, device_id_type=MESH)

    @pl.loop(1, n_tp)
    def _(i):
        pl.semaphore_signal(
            barrier, inc=1, device_id={"tp": lax.rem(tp + i, n_tp)}, device_id_type=MESH
        )

    loads[0].wait()
    loads[1].wait()
    is_base = jnp.full((tile, width), base[0], jnp.int32) == cfg
    for j in range(group):
        mine = rows[tp, pl.ds(j * tile, tile), :].astype(f32)
        masked[j] = jnp.where(is_base, mine, 0.0).astype(bf16)
    mine = rows[tp, pl.ds(seq - TILE, TILE), :].astype(f32)
    probe[...] = jnp.where(is_base[:TILE, :], mine, 0.0).astype(bf16)
    padded = kv.shape[0] // 2
    cap = src.shape[0]
    n_configs = src.shape[1] // n_cfg

    pl.semaphore_wait(barrier, n_cfg - 1 + n_tp - 1)

    def to_cfg(src, dst, which, target):
        return pltpu.make_async_remote_copy(
            src_ref=src,
            dst_ref=dst,
            send_sem=send.at[which],
            recv_sem=recv.at[which],
            device_id={"cfg": target},
            device_id_type=MESH,
        )

    def settle(ref, sem):
        pltpu.make_async_copy(ref, ref, sem).wait()

    def ring(direction, unit):
        hop = unit // 2
        part_no = unit % 2 if direction == 0 else 1 - unit % 2
        sign = 1 if direction == 0 else -1
        slot = lax.rem(tp - sign * hop + n_tp, n_tp)
        piece = rows.at[slot, pl.ds(part_no * half_rows, half_rows)]
        return pltpu.make_async_remote_copy(
            src_ref=piece,
            dst_ref=piece,
            send_sem=ring_send.at[direction, unit],
            recv_sem=ring_recv.at[direction, unit],
            device_id={"tp": lax.rem(tp + sign + n_tp, n_tp)},
            device_id_type=MESH,
        )

    def gains(slot):
        eight = gain_wide[slot]
        return jnp.concatenate([eight[k : k + 1, :] for k in range(per_plane)], axis=1)

    def project(slot, part_no, parts_at_once=1):
        piece = pl.ds(part_no * half_rows, half_rows * parts_at_once)
        wide = rows[slot, piece, :].astype(f32)
        sums[piece, :] += lane_groups(wide * wide)
        normed = (wide * gains(slot)).astype(bf16)
        depth = pl.ds(pl.multiple_of(slot * width, width), width)
        acc[piece, :] += jnp.dot(normed, weights[depth, :], preferred_element_type=f32)

    units = n_tp - 1

    def ring_arrives(unit):
        for direction in (0, 1):
            sign = 1 if direction == 0 else -1
            hop = unit // 2 + 1
            part_no = unit % 2 if direction == 0 else 1 - unit % 2
            slot = lax.rem(tp - sign * hop + n_tp, n_tp)
            piece = rows.at[slot, pl.ds(part_no * half_rows, half_rows)]
            pltpu.make_async_copy(piece, piece, ring_recv.at[direction, unit]).wait()
            if unit + 2 < units:
                ring(direction, unit + 2).start()

    def ring_projects(unit):
        if unit == units - 1:
            project(lax.rem(tp + n_tp // 2, n_tp), 0, 2)
            return
        for direction in (0, 1):
            sign = 1 if direction == 0 else -1
            hop = unit // 2 + 1
            part_no = unit % 2 if direction == 0 else 1 - unit % 2
            project(lax.rem(tp - sign * hop + n_tp, n_tp), part_no)

    for k in range(per_plane):

        @pl.when(cfg != tp * per_plane + k)
        def _():
            to_cfg(
                probe.at[:, pl.ds(k * HD, HD)], probes_met.at[cfg], 2, tp * per_plane + k
            ).start()

    for unit in range(min(2, units)):
        ring(0, unit).start()
        ring(1, unit).start()

    @pl.when(makes_block)
    def _():
        lanes = pl.ds(pl.multiple_of(lax.rem(cfg, per_plane) * HD, HD), HD)
        probes_met[cfg] = probe[:, lanes]

    @pl.loop(1, group)
    def _(i):
        other = lax.rem(place + i, group)
        to_cfg(masked.at[other], row_sums.at[place], 0, turn * group + other).start()

    row_sums[place] = masked[place]
    acc[...] = jnp.zeros_like(acc)
    sums[...] = jnp.zeros_like(sums)
    kv[...] = jnp.zeros_like(kv)
    for load in loads[2:]:
        load.wait()
    span_rows = TILE * 4
    config = lax.broadcasted_iota(jnp.int32, (span_rows, src.shape[1]), 1)
    row_no = lax.broadcasted_iota(jnp.int32, (padded, src.shape[1]), 0)
    asked = [(row_no == src[j : j + 1, :]).astype(f32).astype(bf16) for j in range(cap)]
    is_key = lax.broadcasted_iota(jnp.int32, (span_rows, padded), 0) % TILE < 8

    @pl.loop(0, n_cfg // 4)
    def _(i):
        span = pl.ds(pl.multiple_of(i * span_rows, span_rows), span_rows)
        slot = lax.broadcasted_iota(jnp.int32, (span_rows, src.shape[1]), 0)
        target = i * 4 + lax.shift_right_logical(slot, 4)
        slot = slot & 7
        found = jnp.zeros((span_rows, padded), f32)
        for j in range(cap):
            wanted = jnp.zeros(slot.shape, f32)
            for k in range(n_configs):
                hit = jnp.logical_and(config == target * n_configs + k, slot == k * cap + j)
                wanted = wanted + hit.astype(f32)
            found += lax.dot_general(
                wanted.astype(bf16),
                asked[j],
                (((1,), (1,)), ((), ())),
                preferred_element_type=f32,
            )
        chosen[span, pl.ds(0, padded)] = jnp.where(is_key, found, 0.0).astype(bf16)
        chosen[span, pl.ds(padded, padded)] = jnp.where(is_key, 0.0, found).astype(bf16)

    for z in range(n_tp):
        gain_wide[z] = gain_raw[...].astype(f32)[z * per_plane : (z + 1) * per_plane, :]
    project(tp, 0, 2)

    def probes_meet():
        @pl.when(makes_block)
        def _():
            settle(probes_met.at[pl.ds(0, n_cfg - 1)], recv.at[2])

            def add(source, total):
                return total + probes_met[source].astype(f32)

            total = lax.fori_loop(0, n_cfg, add, jnp.zeros((TILE, HD), f32))
            block[...] = total.astype(bf16)

            @pl.loop(1, n_tp)
            def _(i):
                pltpu.make_async_remote_copy(
                    src_ref=block,
                    dst_ref=block,
                    send_sem=send.at[8],
                    recv_sem=recv.at[8],
                    device_id={"tp": lax.rem(tp + i, n_tp)},
                    device_id_type=MESH,
                ).start()

    def base_meets():
        settle(row_sums.at[pl.ds(0, group - 1)], recv.at[0])
        total = row_sums[0].astype(f32)
        for q in range(1, group):
            total += row_sums[q].astype(f32)
        middle[...] = total.astype(bf16)

        @pl.when(jnp.logical_not(is_holder))
        def _():
            to_cfg(middle, landed.at[turn], 7, holder).start()

        @pl.when(is_holder)
        def _():
            landed[turn] = middle[...]

    def place_slots():
        slots = n_cfg * 8
        source = lax.broadcasted_iota(jnp.int32, (n_cfg, slots), 0)
        slot = lax.broadcasted_iota(jnp.int32, (n_cfg, slots), 1)
        spread = (source == lax.shift_right_logical(slot, 3)).astype(f32).astype(bf16)
        position = lax.broadcasted_iota(jnp.int32, (seq, slots), 0).astype(f32) + 1.0
        slot_of = lax.broadcasted_iota(jnp.int32, (8, slots), 1) & 7
        row_id = lax.broadcasted_iota(jnp.int32, (8, slots), 0)
        order = lax.broadcasted_iota(jnp.int32, (cap, n_cfg), 0)
        down = lax.broadcasted_iota(jnp.int32, (seq, padded), 0)
        diagonal = (down == lax.broadcasted_iota(jnp.int32, (seq, padded), 1)).astype(f32)
        for i in range(n_configs):
            valid = order < used[i : i + 1, :]
            goal = jnp.where(valid, dst[i] + 1, 0).astype(f32)
            goal = jnp.concatenate([goal, jnp.zeros((8 - cap, n_cfg), f32)], axis=0)
            wide = jnp.dot(goal.astype(bf16), spread, preferred_element_type=f32)
            mine = jnp.logical_and(slot_of == row_id + i * cap, row_id < cap)
            goal = jnp.sum(jnp.where(mine, wide, 0.0), axis=0, keepdims=True)
            onehot = (position == goal).astype(f32)
            free = 1.0 - jnp.max(onehot, axis=1, keepdims=True)
            placed[pl.ds(i * seq, seq), pl.ds(0, slots)] = onehot.astype(bf16)
            placed[pl.ds(i * seq, seq), pl.ds(slots, padded)] = (diagonal * free).astype(bf16)
        pltpu.make_async_copy(placed, splices, load_sem.at[3]).start()

    def base_arrives():
        @pl.when(is_holder)
        def _():
            settle(landed.at[pl.ds(0, rings - 1)], recv.at[7])
            total = landed[0].astype(f32)
            for y in range(1, rings):
                total += landed[y].astype(f32)
            base_rows[tp] = total.astype(bf16)

            @pl.loop(1, n_tp)
            def _(i):
                pltpu.make_async_remote_copy(
                    src_ref=base_rows.at[tp],
                    dst_ref=base_rows.at[tp],
                    send_sem=send.at[1],
                    recv_sem=recv.at[1],
                    device_id={"tp": lax.rem(tp + i, n_tp)},
                    device_id_type=MESH,
                ).start()

    def base_projects():
        @pl.when(is_holder)
        def _():
            settle(base_rows.at[pl.ds(0, n_tp - 1)], recv.at[1])

            def add(z, state):
                total, squares = state
                wide = base_rows[z].astype(f32)
                normed = (wide * gains(z)).astype(bf16)
                depth = pl.ds(pl.multiple_of(z * width, width), width)
                total += jnp.dot(normed, weights[depth, :], preferred_element_type=f32)
                return total, squares + lane_groups(wide * wide)

            total, squares = lax.fori_loop(
                0, n_tp, add, (jnp.zeros((tile, 2 * HD), f32), jnp.zeros((tile, HD), f32))
            )
            scale = lax.rsqrt(jnp.sum(squares, axis=1, keepdims=True) / model + EPSILON)
            my_base_kv[...] = (total * scale).astype(bf16)

            @pl.loop(0, rings - 1)
            def _(i):
                other = lax.rem(turn + outward(i, rings), rings)
                to_cfg(my_base_kv, my_base_kv, 3, other * group + place).start()

    def base_spreads():
        @pl.when(jnp.logical_not(is_holder))
        def _():
            settle(my_base_kv, recv.at[3])

        @pl.loop(1, group)
        def _(i):
            other = lax.rem(place + i, group)
            to_cfg(my_base_kv, base_kv.at[place], 9, turn * group + other).start()

        pltpu.make_async_copy(my_base_kv, base_kv.at[place], load_sem.at[0]).start()

    def query_parts():
        @pl.when(jnp.logical_not(makes_block))
        def _():
            settle(block, recv.at[8])

        wide = block[...].astype(f32)[TILE - 8 :, :]
        own_gain = gain_wide[cfg // per_plane]
        pick = lax.broadcasted_iota(jnp.int32, own_gain.shape, 0) == lax.rem(cfg, per_plane)
        own_gain = jnp.sum(jnp.where(pick, own_gain, 0.0), axis=0, keepdims=True)
        normed = (wide * own_gain).astype(bf16)
        total = jnp.dot(normed, wq[...], preferred_element_type=f32)
        squares = wide * wide
        for h in range(heads):
            part[h, pl.ds(0, 8), :] = total[:, h * HD : (h + 1) * HD]
            part[h, pl.ds(8, 8), :] = squares
        for h in range(heads):

            @pl.when(cfg != owner(h))
            def _():
                to_cfg(part.at[h], parts.at[cfg], 4, owner(h)).start()

        @pl.when(is_owner)
        def _():
            parts[cfg] = part[my_head]

    def query_sums():
        @pl.when(is_owner)
        def _():
            settle(parts.at[pl.ds(0, n_cfg - 1)], recv.at[4])

            def add(s, total):
                return total + parts[s]

            total = lax.fori_loop(0, n_cfg, add, jnp.zeros((TILE, HD), f32))
            scale = lax.rsqrt(jnp.sum(total[8:], axis=1, keepdims=True) / model + EPSILON)
            my_queries[...] = rotate(
                total[:8] * scale, rope[0, pl.ds(seq - 8, 8), :], rope[1, pl.ds(seq - 8, 8), :]
            )

            pltpu.make_async_copy(my_queries, queries.at[my_head], load_sem.at[1]).start()

            @pl.loop(0, n_cfg - 1)
            def _(i):
                to_cfg(my_queries, queries.at[my_head], 5, peer(i)).start()

    beside = [
        (probes_meet, base_meets),
        (base_arrives, query_parts),
        (place_slots,),
        (base_projects,),
        (query_sums,),
        (base_spreads,),
    ]
    for unit in range(max(units, len(beside))):
        if unit < units:
            ring_arrives(unit)
        if unit < len(beside):
            for stage in beside[unit]:
                stage()
        if unit < units:
            ring_projects(unit)

    scale = lax.rsqrt(jnp.sum(sums[...], axis=1, keepdims=True) / model + EPSILON)
    scaled = (acc[...] * scale).astype(bf16)
    kv[pl.ds(0, seq), :] = scaled[:, :HD]
    kv[pl.ds(padded, seq), :] = scaled[:, HD:]
    picked = jnp.dot(chosen[...], kv[...], preferred_element_type=f32).astype(bf16)
    outgoing[...] = picked.reshape(n_cfg, TILE, HD)

    @pl.loop(0, n_cfg - 1)
    def _(i):
        target = peer(i)
        to_cfg(outgoing.at[target], arrived.at[cfg], 6, target).start()

    own = pltpu.make_async_copy(outgoing.at[cfg], arrived.at[cfg], load_sem.at[2])
    own.start()

    def both(condition, if_true, if_false):
        pl.when(condition)(if_true)
        pl.when(jnp.logical_not(condition))(if_false)

    for unit in range(units):
        for direction in (0, 1):
            ring(direction, unit).wait_send()
    settle(masked.at[pl.ds(0, group - 1)], send.at[0])

    @pl.when(jnp.logical_not(is_holder))
    def _():
        settle(middle, send.at[7])

    @pl.when(is_holder)
    def _():
        settle(base_rows.at[pl.ds(0, n_tp - 1)], send.at[1])
        settle(base_kv.at[pl.ds(0, rings - 1)], send.at[3])

    both(
        makes_block,
        lambda: settle(probes_met.at[pl.ds(0, per_plane - 1)], send.at[2]),
        lambda: settle(probes_met.at[pl.ds(0, per_plane)], send.at[2]),
    )

    @pl.when(makes_block)
    def _():
        settle(probes_met.at[pl.ds(0, n_tp - 1)], send.at[8])

    both(
        is_owner,
        lambda: settle(part.at[pl.ds(0, heads - 1)], send.at[4]),
        lambda: settle(part, send.at[4]),
    )
    settle(base_kv.at[pl.ds(0, group - 1)], send.at[9])
    settle(base_kv.at[pl.ds(0, group - 1)], recv.at[9])
    both(
        is_owner,
        lambda: settle(queries.at[pl.ds(0, heads - 1)], recv.at[5]),
        lambda: settle(queries, recv.at[5]),
    )

    @pl.when(is_owner)
    def _():
        settle(arrived.at[pl.ds(0, n_cfg - 1)], send.at[5])

    settle(outgoing.at[pl.ds(0, n_cfg - 1)], send.at[6])
    settle(arrived.at[pl.ds(0, n_cfg - 1)], recv.at[6])
    own.wait()
    pltpu.make_async_copy(placed, splices, load_sem.at[3]).wait()

    pltpu.make_async_copy(my_base_kv, base_kv.at[place], load_sem.at[0]).wait()

    @pl.when(is_owner)
    def _():
        pltpu.make_async_copy(my_queries, queries.at[my_head], load_sem.at[1]).wait()


def attend_kernel(
    arrived_in,
    base_in,
    queries_in,
    splices_in,
    rope_in,
    attended,
    keys,
    values,
    arrived,
    base_kv,
    queries,
    splices,
    rope,
    sem,
):
    loads = [
        pltpu.make_async_copy(source, target, sem.at[i])
        for i, (source, target) in enumerate(
            (
                (splices_in, splices),
                (arrived_in, arrived),
                (base_in, base_kv),
                (rope_in, rope),
                (queries_in, queries),
            )
        )
    ]
    for load in loads:
        load.start()
    n_configs, seq = keys.shape[0], keys.shape[1]
    heads, n_cfg = queries.shape[0], arrived.shape[0]
    probe_row = lax.broadcasted_iota(jnp.int32, (heads * 8, seq), 0) & 7
    causal = lax.broadcasted_iota(jnp.int32, (heads * 8, seq), 1) <= seq - 8 + probe_row
    slots = n_cfg * 8
    for load in loads:
        load.wait()
    probes = queries[...].reshape(heads * 8, HD).astype(bf16)
    spliced = arrived[...].astype(f32)
    taken_rows = jnp.concatenate(
        [spliced[:, :8, :].reshape(slots, HD), spliced[:, 8:, :].reshape(slots, HD)], axis=1
    )
    base_all = base_kv[...].astype(f32).reshape(seq, 2 * HD)
    none = jnp.zeros((splices.shape[1] - slots - seq, 2 * HD), f32)
    taken_rows = jnp.concatenate([taken_rows, base_all, none], axis=0).astype(bf16)
    for i in range(n_configs):
        splice = splices[pl.ds(i * seq, seq), :]
        mixed = jnp.dot(splice, taken_rows, preferred_element_type=f32)
        key = rotate(mixed[:, :HD], rope[0], rope[1]).astype(bf16)
        value = mixed[:, HD:].astype(bf16)
        keys[i] = key
        values[i] = value
        scores = lax.dot_general(
            probes, key, (((1,), (1,)), ((), ())), preferred_element_type=f32
        ) * HD ** (-0.5)
        scores = jnp.where(causal, scores, -1e30)
        top = jnp.max(scores, axis=1, keepdims=True)
        grown = jnp.exp(scores - top)
        probs = (grown / jnp.sum(grown, axis=1, keepdims=True)).astype(bf16)
        out = jnp.dot(probs, value, preferred_element_type=f32)
        for h in range(heads):
            attended[i, :, h * HD : (h + 1) * HD] = out[h * 8 + 8 - PROBE : h * 8 + 8, :].astype(bf16)


def body(n_cfg, n_tp, pool, base_run, gain, w_key, w_value, w_query, src_pos, dst_pos, counts):
    seq, width = pool.shape[1], pool.shape[2]
    n_configs, cap = dst_pos.shape[0], dst_pos.shape[2]
    heads = w_query.shape[1] // HD
    group = 1 << (n_cfg.bit_length() // 2)
    tile = seq // group
    padded = -(-seq // HD) * HD
    vmem, anywhere = pl.BlockSpec(memory_space=pltpu.VMEM), pl.BlockSpec(memory_space=pl.ANY)
    dma, hops = pltpu.SemaphoreType.DMA, n_tp - 1
    table = jnp.asarray(rope_tables(0, seq))
    arrived, base_kv, queries, splices = pl.pallas_call(
        functools.partial(sweep_kernel, n_cfg, n_tp),
        out_shape=(
            jax.ShapeDtypeStruct((n_cfg, TILE, HD), bf16),
            jax.ShapeDtypeStruct((group, tile, 2 * HD), bf16),
            jax.ShapeDtypeStruct((heads, 8, HD), f32),
            jax.ShapeDtypeStruct((n_configs * seq, n_cfg * 8 + padded), bf16),
        ),
        in_specs=[anywhere] * 10,
        out_specs=(anywhere,) * 4,
        scratch_shapes=[
            pltpu.SMEM((1,), jnp.int32),
            pltpu.VMEM((n_tp, seq, width), bf16),
            pltpu.VMEM((n_tp * width, 2 * HD), bf16),
            pltpu.VMEM(w_query.shape, bf16),
            pltpu.VMEM((n_cfg, HD), bf16),
            pltpu.VMEM((n_tp, n_cfg // n_tp, HD), f32),
            pltpu.VMEM((cap, n_configs * n_cfg), jnp.int32),
            pltpu.VMEM((n_configs, cap, n_cfg), jnp.int32),
            pltpu.VMEM((n_configs, n_cfg), jnp.int32),
            pltpu.VMEM((2, seq, HD), f32),
            pltpu.VMEM((n_configs * seq, n_cfg * 8 + padded), bf16),
            pltpu.VMEM((group, tile, width), bf16),
            pltpu.VMEM((group, tile, width), bf16),
            pltpu.VMEM((tile, width), bf16),
            pltpu.VMEM((n_cfg // group, tile, width), bf16),
            pltpu.VMEM((n_tp, tile, width), bf16),
            pltpu.VMEM((TILE, width), bf16),
            pltpu.VMEM((n_cfg, TILE, HD), bf16),
            pltpu.VMEM((TILE, HD), bf16),
            pltpu.VMEM((heads, TILE, HD), f32),
            pltpu.VMEM((n_cfg, TILE, HD), f32),
            pltpu.VMEM((8, HD), f32),
            pltpu.VMEM((tile, 2 * HD), bf16),
            pltpu.VMEM((n_cfg * TILE, 2 * padded), bf16),
            pltpu.VMEM((2 * padded, HD), bf16),
            pltpu.VMEM((n_cfg, TILE, HD), bf16),
            pltpu.VMEM((seq, 2 * HD), f32),
            pltpu.VMEM((seq, HD), f32),
            dma((11,)),
            dma((2, hops)),
            dma((2, hops)),
            dma((10,)),
            dma((10,)),
        ],
        compiler_params=pltpu.CompilerParams(
            collective_id=0, has_side_effects=True, vmem_limit_bytes=60 << 20
        ),
    )(
        pool[0],
        base_run,
        gain.reshape(n_cfg, HD),
        w_key,
        w_value,
        w_query,
        jnp.transpose(src_pos[:, 0, :], (1, 0)),
        table,
        jnp.transpose(dst_pos, (0, 2, 1)),
        counts,
    )
    return pl.pallas_call(
        attend_kernel,
        out_shape=(
            jax.ShapeDtypeStruct((n_configs, PROBE, heads * HD), bf16),
            jax.ShapeDtypeStruct((n_configs, seq, HD), bf16),
            jax.ShapeDtypeStruct((n_configs, seq, HD), bf16),
        ),
        in_specs=[anywhere] * 5,
        out_specs=(vmem, vmem, vmem),
        scratch_shapes=[
            pltpu.VMEM(arrived.shape, bf16),
            pltpu.VMEM(base_kv.shape, bf16),
            pltpu.VMEM(queries.shape, f32),
            pltpu.VMEM(splices.shape, bf16),
            pltpu.VMEM(table.shape, f32),
            dma((5,)),
        ],
        compiler_params=pltpu.CompilerParams(vmem_limit_bytes=60 << 20),
    )(arrived, base_kv, queries, splices, table)


def solution(mesh):
    placed = (
        P("cfg", None, "tp"),
        P(),
        P(),
        P(None, "tp"),
        P(None, "tp"),
        P("cfg", "tp"),
        P(None, "cfg", None),
        P("cfg", None, None),
        P("cfg", None),
    )
    return jax.shard_map(
        functools.partial(body, mesh.shape["cfg"], mesh.shape["tp"]),
        mesh=mesh,
        in_specs=placed,
        out_specs=(P("cfg", None, "tp"), P("cfg", None, "tp"), P("cfg", None, "tp")),
        check_vma=False,
    )
```

```python
import functools
import math

import jax
import jax.numpy as jnp
import numpy as np
from jax import lax
from jax.experimental import pallas as pl
from jax.experimental.pallas import tpu as pltpu
from jax.sharding import PartitionSpec as P

HD = 128
PROBE = 4
TILE = 16
ROPE_BASE = 500000.0
EPSILON = 1e-05
MESH = pl.DeviceIdType.MESH
f32 = jnp.float32
bf16 = jnp.bfloat16


def rope_tables(first, count):
    half = HD // 2
    freq = np.exp(np.arange(half, dtype=np.float64) * (-2.0 * math.log(ROPE_BASE) / HD))
    angles = np.arange(first, first + count, dtype=np.float64)[:, None] * freq[None, :]
    cosine, sine = np.cos(angles), np.sin(angles)
    return np.stack(
        [np.concatenate([cosine, cosine], 1), np.concatenate([-sine, sine], 1)]
    ).astype(np.float32)


def rotate(rows, cosine, sine):
    return rows * cosine + pltpu.roll(rows, HD // 2, 1) * sine


def lane_groups(squares):
    total = squares[:, :HD]
    for k in range(1, squares.shape[1] // HD):
        total = total + squares[:, k * HD : (k + 1) * HD]
    return total


def sweep_kernel(
    n_cfg,
    n_tp,
    pool,
    base_run,
    gain,
    w_key,
    w_value,
    w_query,
    src_pos,
    rope_table,
    dst_pos,
    counts,
    arrived,
    base_kv,
    queries,
    splices,
    base,
    rows,
    weights,
    wq,
    gain_raw,
    gain_wide,
    src,
    dst,
    used,
    rope,
    placed,
    masked,
    row_sums,
    middle,
    landed,
    base_rows,
    probe,
    probes_met,
    block,
    part,
    parts,
    my_queries,
    my_base_kv,
    chosen,
    kv,
    outgoing,
    acc,
    sums,
    load_sem,
    ring_send,
    ring_recv,
    send,
    recv,
):
    cfg, tp = lax.axis_index("cfg"), lax.axis_index("tp")
    seq, width = rows.shape[1], rows.shape[2]
    half_rows = seq // 2
    model = n_tp * width
    heads = queries.shape[0]
    group, tile = masked.shape[0], masked.shape[1]
    rings = n_cfg // group
    place, turn = lax.rem(cfg, group), cfg // group
    pieces = tile // 8

    def holder(piece):
        return lax.rem(place + 3 * piece, rings) * group + place

    held = [cfg == holder(piece) for piece in range(pieces)]
    is_holder = functools.reduce(jnp.logical_or, held)
    my_piece = sum(piece * hit.astype(jnp.int32) for piece, hit in enumerate(held))

    def owner(head):
        return (head + rings // 2) % rings * group + head

    is_owner = jnp.logical_and(turn == lax.rem(place + rings // 2, rings), place < heads)
    my_head = lax.rem(place, heads)
    per_plane = n_cfg // n_tp
    makes_block = cfg // per_plane == tp

    loads = [
        pltpu.make_async_copy(source, target, load_sem.at[i])
        for i, (source, target) in enumerate(
            (
                (pool, rows.at[tp]),
                (base_run, base),
                (gain, gain_raw),
                (w_key, weights.at[:, pl.ds(0, HD)]),
                (w_value, weights.at[:, pl.ds(HD, HD)]),
                (w_query, wq),
                (src_pos, src),
                (rope_table, rope),
                (dst_pos, dst),
                (counts, used),
            )
        )
    ]
    for load in loads:
        load.start()

    def outward(i, size):
        step = lax.div(i + 1, 2)
        return lax.rem(size // 2 + jnp.where(lax.rem(i, 2) == 0, step, size - step), size)

    def peer(i):
        across = lax.rem(i, group)
        y = lax.rem(turn + outward(lax.div(i, group), rings), rings)
        x = lax.rem(lax.div(place, 2) + outward(lax.div(across, 2), group // 2), group // 2)
        core = lax.rem(place + 1 - lax.rem(across, 2), 2)
        return y * group + x * 2 + core

    barrier = pltpu.get_barrier_semaphore()

    @pl.loop(1, n_tp)
    def _(i):
        pl.semaphore_signal(
            barrier, inc=1, device_id={"tp": lax.rem(tp + i, n_tp)}, device_id_type=MESH
        )

    @pl.loop(0, n_cfg - 1)
    def _(i):
        pl.semaphore_signal(barrier, inc=1, device_id={"cfg": peer(i)}, device_id_type=MESH)

    loads[0].wait()
    loads[1].wait()
    is_base = jnp.full((tile, width), base[0], jnp.int32) == cfg
    for j in range(group):
        mine = rows[tp, pl.ds(j * tile, tile), :].astype(f32)
        masked[j] = jnp.where(is_base, mine, 0.0).astype(bf16)
    mine = rows[tp, pl.ds(seq - TILE, TILE), :].astype(f32)
    probe[...] = jnp.where(is_base[:TILE, :], mine, 0.0).astype(bf16)
    padded = kv.shape[0] // 2
    cap = src.shape[0]
    n_configs = src.shape[1] // n_cfg

    pl.semaphore_wait(barrier, n_cfg - 1 + n_tp - 1)

    def to_cfg(src, dst, which, target):
        return pltpu.make_async_remote_copy(
            src_ref=src,
            dst_ref=dst,
            send_sem=send.at[which],
            recv_sem=recv.at[which],
            device_id={"cfg": target},
            device_id_type=MESH,
        )

    def both(condition, if_true, if_false):
        pl.when(condition)(if_true)
        pl.when(jnp.logical_not(condition))(if_false)

    def settle(ref, sem):
        pltpu.make_async_copy(ref, ref, sem).wait()

    def ring(direction, unit):
        hop = unit // 2
        part_no = unit % 2 if direction == 0 else 1 - unit % 2
        sign = 1 if direction == 0 else -1
        slot = lax.rem(tp - sign * hop + n_tp, n_tp)
        piece = rows.at[slot, pl.ds(part_no * half_rows, half_rows)]
        return pltpu.make_async_remote_copy(
            src_ref=piece,
            dst_ref=piece,
            send_sem=ring_send.at[direction, unit],
            recv_sem=ring_recv.at[direction, unit],
            device_id={"tp": lax.rem(tp + sign + n_tp, n_tp)},
            device_id_type=MESH,
        )

    def gains(slot):
        eight = gain_wide[slot]
        return jnp.concatenate([eight[k : k + 1, :] for k in range(per_plane)], axis=1)

    def project(slot, part_no, parts_at_once=1):
        piece = pl.ds(part_no * half_rows, half_rows * parts_at_once)
        wide = rows[slot, piece, :].astype(f32)
        sums[piece, :] += lane_groups(wide * wide)
        normed = (wide * gains(slot)).astype(bf16)
        depth = pl.ds(pl.multiple_of(slot * width, width), width)
        acc[piece, :] += jnp.dot(normed, weights[depth, :], preferred_element_type=f32)

    units = n_tp - 1

    def ring_arrives(unit):
        for direction in (0, 1):
            sign = 1 if direction == 0 else -1
            hop = unit // 2 + 1
            part_no = unit % 2 if direction == 0 else 1 - unit % 2
            slot = lax.rem(tp - sign * hop + n_tp, n_tp)
            piece = rows.at[slot, pl.ds(part_no * half_rows, half_rows)]
            pltpu.make_async_copy(piece, piece, ring_recv.at[direction, unit]).wait()
            if unit + 2 < units:
                ring(direction, unit + 2).start()

    def ring_projects(unit):
        if unit == units - 1:
            project(lax.rem(tp + n_tp // 2, n_tp), 0, 2)
            return
        for direction in (0, 1):
            sign = 1 if direction == 0 else -1
            hop = unit // 2 + 1
            part_no = unit % 2 if direction == 0 else 1 - unit % 2
            project(lax.rem(tp - sign * hop + n_tp, n_tp), part_no)

    for k in range(per_plane):

        @pl.when(cfg != tp * per_plane + k)
        def _():
            to_cfg(
                probe.at[:, pl.ds(k * HD, HD)], probes_met.at[cfg], 2, tp * per_plane + k
            ).start()

    for unit in range(min(2, units)):
        ring(0, unit).start()
        ring(1, unit).start()

    @pl.when(makes_block)
    def _():
        lanes = pl.ds(pl.multiple_of(lax.rem(cfg, per_plane) * HD, HD), HD)
        probes_met[cfg] = probe[:, lanes]

    @pl.loop(1, group)
    def _(i):
        other = lax.rem(place + i, group)
        to_cfg(masked.at[other], row_sums.at[place], 0, turn * group + other).start()

    row_sums[place] = masked[place]
    acc[...] = jnp.zeros_like(acc)
    sums[...] = jnp.zeros_like(sums)
    kv[...] = jnp.zeros_like(kv)
    for load in loads[2:]:
        load.wait()
    span_rows = TILE * 4
    config = lax.broadcasted_iota(jnp.int32, (span_rows, src.shape[1]), 1)
    row_no = lax.broadcasted_iota(jnp.int32, (padded, src.shape[1]), 0)
    asked = [(row_no == src[j : j + 1, :]).astype(f32).astype(bf16) for j in range(cap)]
    is_key = lax.broadcasted_iota(jnp.int32, (span_rows, padded), 0) % TILE < 8

    @pl.loop(0, n_cfg // 4)
    def _(i):
        span = pl.ds(pl.multiple_of(i * span_rows, span_rows), span_rows)
        slot = lax.broadcasted_iota(jnp.int32, (span_rows, src.shape[1]), 0)
        target = i * 4 + lax.shift_right_logical(slot, 4)
        slot = slot & 7
        found = jnp.zeros((span_rows, padded), f32)
        for j in range(cap):
            wanted = jnp.zeros(slot.shape, f32)
            for k in range(n_configs):
                hit = jnp.logical_and(config == target * n_configs + k, slot == k * cap + j)
                wanted = wanted + hit.astype(f32)
            found += lax.dot_general(
                wanted.astype(bf16),
                asked[j],
                (((1,), (1,)), ((), ())),
                preferred_element_type=f32,
            )
        chosen[span, pl.ds(0, padded)] = jnp.where(is_key, found, 0.0).astype(bf16)
        chosen[span, pl.ds(padded, padded)] = jnp.where(is_key, 0.0, found).astype(bf16)

    for z in range(n_tp):
        gain_wide[z] = gain_raw[...].astype(f32)[z * per_plane : (z + 1) * per_plane, :]
    project(tp, 0, 2)

    def probes_meet():
        @pl.when(makes_block)
        def _():
            settle(probes_met.at[pl.ds(0, n_cfg - 1)], recv.at[2])

            def add(source, total):
                return total + probes_met[source].astype(f32)

            total = lax.fori_loop(0, n_cfg, add, jnp.zeros((TILE, HD), f32))
            block[...] = total.astype(bf16)

            @pl.loop(1, n_tp)
            def _(i):
                pltpu.make_async_remote_copy(
                    src_ref=block,
                    dst_ref=block,
                    send_sem=send.at[8],
                    recv_sem=recv.at[8],
                    device_id={"tp": lax.rem(tp + i, n_tp)},
                    device_id_type=MESH,
                ).start()

    def base_meets():
        settle(row_sums.at[pl.ds(0, group - 1)], recv.at[0])
        total = row_sums[0].astype(f32)
        for q in range(1, group):
            total += row_sums[q].astype(f32)
        for piece in range(pieces):
            middle[piece] = total[piece * 8 : (piece + 1) * 8, :].astype(bf16)

            @pl.when(jnp.logical_not(held[piece]))
            def _():
                to_cfg(middle.at[piece], landed.at[turn], 7, holder(piece)).start()

            @pl.when(held[piece])
            def _():
                landed[turn] = middle[piece]

    def place_slots():
        slots = n_cfg * 8
        source = lax.broadcasted_iota(jnp.int32, (n_cfg, slots), 0)
        slot = lax.broadcasted_iota(jnp.int32, (n_cfg, slots), 1)
        spread = (source == lax.shift_right_logical(slot, 3)).astype(f32).astype(bf16)
        position = lax.broadcasted_iota(jnp.int32, (seq, slots), 0).astype(f32) + 1.0
        slot_of = lax.broadcasted_iota(jnp.int32, (8, slots), 1) & 7
        row_id = lax.broadcasted_iota(jnp.int32, (8, slots), 0)
        order = lax.broadcasted_iota(jnp.int32, (cap, n_cfg), 0)
        down = lax.broadcasted_iota(jnp.int32, (seq, padded), 0)
        diagonal = (down == lax.broadcasted_iota(jnp.int32, (seq, padded), 1)).astype(f32)
        for i in range(n_configs):
            valid = order < used[i : i + 1, :]
            goal = jnp.where(valid, dst[i] + 1, 0).astype(f32)
            goal = jnp.concatenate([goal, jnp.zeros((8 - cap, n_cfg), f32)], axis=0)
            wide = jnp.dot(goal.astype(bf16), spread, preferred_element_type=f32)
            mine = jnp.logical_and(slot_of == row_id + i * cap, row_id < cap)
            goal = jnp.sum(jnp.where(mine, wide, 0.0), axis=0, keepdims=True)
            onehot = (position == goal).astype(f32)
            free = 1.0 - jnp.max(onehot, axis=1, keepdims=True)
            placed[pl.ds(i * seq, seq), pl.ds(0, slots)] = onehot.astype(bf16)
            placed[pl.ds(i * seq, seq), pl.ds(slots, padded)] = (diagonal * free).astype(bf16)
        pltpu.make_async_copy(placed, splices, load_sem.at[3]).start()

    def base_arrives():
        @pl.when(is_holder)
        def _():
            settle(landed.at[pl.ds(0, rings - 1)], recv.at[7])
            total = landed[0].astype(f32)
            for y in range(1, rings):
                total += landed[y].astype(f32)
            base_rows[tp] = total.astype(bf16)

            @pl.loop(1, n_tp)
            def _(i):
                pltpu.make_async_remote_copy(
                    src_ref=base_rows.at[tp],
                    dst_ref=base_rows.at[tp],
                    send_sem=send.at[1],
                    recv_sem=recv.at[1],
                    device_id={"tp": lax.rem(tp + i, n_tp)},
                    device_id_type=MESH,
                ).start()

    def base_projects():
        @pl.when(is_holder)
        def _():
            settle(base_rows.at[pl.ds(0, n_tp - 1)], recv.at[1])

            def add(z, state):
                total, squares = state
                wide = base_rows[z].astype(f32)
                normed = (wide * gains(z)).astype(bf16)
                depth = pl.ds(pl.multiple_of(z * width, width), width)
                total += jnp.dot(normed, weights[depth, :], preferred_element_type=f32)
                return total, squares + lane_groups(wide * wide)

            total, squares = lax.fori_loop(
                0, n_tp, add, (jnp.zeros((8, 2 * HD), f32), jnp.zeros((8, HD), f32))
            )
            scale = lax.rsqrt(jnp.sum(squares, axis=1, keepdims=True) / model + EPSILON)
            my_base_kv[my_piece] = (total * scale).astype(bf16)

            @pl.loop(0, rings - 1)
            def _(i):
                other = lax.rem(turn + outward(i, rings), rings)
                mine = my_base_kv.at[my_piece]
                to_cfg(mine, mine, 3, other * group + place).start()

    def base_spreads():
        both(
            is_holder,
            lambda: settle(my_base_kv.at[pl.ds(0, pieces - 1)], recv.at[3]),
            lambda: settle(my_base_kv, recv.at[3]),
        )

        @pl.loop(1, group)
        def _(i):
            other = lax.rem(place + i, group)
            to_cfg(my_base_kv, base_kv.at[place], 9, turn * group + other).start()

        pltpu.make_async_copy(my_base_kv, base_kv.at[place], load_sem.at[0]).start()

    def query_parts():
        @pl.when(jnp.logical_not(makes_block))
        def _():
            settle(block, recv.at[8])

        wide = block[...].astype(f32)[TILE - 8 :, :]
        own_gain = gain_wide[cfg // per_plane]
        pick = lax.broadcasted_iota(jnp.int32, own_gain.shape, 0) == lax.rem(cfg, per_plane)
        own_gain = jnp.sum(jnp.where(pick, own_gain, 0.0), axis=0, keepdims=True)
        normed = (wide * own_gain).astype(bf16)
        total = jnp.dot(normed, wq[...], preferred_element_type=f32)
        squares = wide * wide
        for h in range(heads):
            part[h, pl.ds(0, 8), :] = total[:, h * HD : (h + 1) * HD]
            part[h, pl.ds(8, 8), :] = squares
        for h in range(heads):

            @pl.when(cfg != owner(h))
            def _():
                to_cfg(part.at[h], parts.at[cfg], 4, owner(h)).start()

        @pl.when(is_owner)
        def _():
            parts[cfg] = part[my_head]

    def query_sums():
        @pl.when(is_owner)
        def _():
            settle(parts.at[pl.ds(0, n_cfg - 1)], recv.at[4])

            def add(s, total):
                return total + parts[s]

            total = lax.fori_loop(0, n_cfg, add, jnp.zeros((TILE, HD), f32))
            scale = lax.rsqrt(jnp.sum(total[8:], axis=1, keepdims=True) / model + EPSILON)
            my_queries[...] = rotate(
                total[:8] * scale, rope[0, pl.ds(seq - 8, 8), :], rope[1, pl.ds(seq - 8, 8), :]
            )

            pltpu.make_async_copy(my_queries, queries.at[my_head], load_sem.at[1]).start()

            @pl.loop(0, n_cfg - 1)
            def _(i):
                to_cfg(my_queries, queries.at[my_head], 5, peer(i)).start()

    beside = [
        (probes_meet, base_meets),
        (base_arrives, query_parts),
        (place_slots,),
        (base_projects,),
        (query_sums,),
        (base_spreads,),
    ]
    for unit in range(max(units, len(beside))):
        if unit < units:
            ring_arrives(unit)
        if unit < len(beside):
            for stage in beside[unit]:
                stage()
        if unit < units:
            ring_projects(unit)

    scale = lax.rsqrt(jnp.sum(sums[...], axis=1, keepdims=True) / model + EPSILON)
    scaled = (acc[...] * scale).astype(bf16)
    kv[pl.ds(0, seq), :] = scaled[:, :HD]
    kv[pl.ds(padded, seq), :] = scaled[:, HD:]

    @pl.loop(0, rings)
    def _(step):
        first = lax.rem(turn + outward(step, rings), rings) * group
        span = pl.ds(pl.multiple_of(first * TILE, TILE * group), TILE * group)
        picked = jnp.dot(chosen[span, :], kv[...], preferred_element_type=f32).astype(bf16)
        outgoing[pl.ds(first, group)] = picked.reshape(group, TILE, HD)

        @pl.loop(0, group)
        def _(across):
            x = lax.rem(lax.div(place, 2) + outward(lax.div(across, 2), group // 2), group // 2)
            target = first + x * 2 + lax.rem(place + 1 - lax.rem(across, 2), 2)

            @pl.when(target != cfg)
            def _():
                to_cfg(outgoing.at[target], arrived.at[cfg], 6, target).start()

    own = pltpu.make_async_copy(outgoing.at[cfg], arrived.at[cfg], load_sem.at[2])
    own.start()

    for unit in range(units):
        for direction in (0, 1):
            ring(direction, unit).wait_send()
    settle(masked.at[pl.ds(0, group - 1)], send.at[0])

    both(
        is_holder,
        lambda: settle(middle.at[pl.ds(0, pieces - 1)], send.at[7]),
        lambda: settle(middle, send.at[7]),
    )

    @pl.when(is_holder)
    def _():
        settle(base_rows.at[pl.ds(0, n_tp - 1)], send.at[1])
        settle(base_kv.at[pl.ds(0, rings - 1), 0], send.at[3])

    both(
        makes_block,
        lambda: settle(probes_met.at[pl.ds(0, per_plane - 1)], send.at[2]),
        lambda: settle(probes_met.at[pl.ds(0, per_plane)], send.at[2]),
    )

    @pl.when(makes_block)
    def _():
        settle(probes_met.at[pl.ds(0, n_tp - 1)], send.at[8])

    both(
        is_owner,
        lambda: settle(part.at[pl.ds(0, heads - 1)], send.at[4]),
        lambda: settle(part, send.at[4]),
    )
    settle(base_kv.at[pl.ds(0, group - 1)], send.at[9])
    settle(base_kv.at[pl.ds(0, group - 1)], recv.at[9])
    both(
        is_owner,
        lambda: settle(queries.at[pl.ds(0, heads - 1)], recv.at[5]),
        lambda: settle(queries, recv.at[5]),
    )

    @pl.when(is_owner)
    def _():
        settle(arrived.at[pl.ds(0, n_cfg - 1)], send.at[5])

    settle(outgoing.at[pl.ds(0, n_cfg - 1)], send.at[6])
    settle(arrived.at[pl.ds(0, n_cfg - 1)], recv.at[6])
    own.wait()
    pltpu.make_async_copy(placed, splices, load_sem.at[3]).wait()

    pltpu.make_async_copy(my_base_kv, base_kv.at[place], load_sem.at[0]).wait()

    @pl.when(is_owner)
    def _():
        pltpu.make_async_copy(my_queries, queries.at[my_head], load_sem.at[1]).wait()


def attend_kernel(
    arrived_in,
    base_in,
    queries_in,
    splices_in,
    rope_in,
    attended_out,
    keys_out,
    values_out,
    attended,
    keys,
    values,
    arrived,
    base_kv,
    queries,
    splices,
    rope,
    sem,
):
    loads = [
        pltpu.make_async_copy(source, target, sem.at[i])
        for i, (source, target) in enumerate(
            (
                (splices_in, splices),
                (arrived_in, arrived),
                (base_in, base_kv),
                (rope_in, rope),
                (queries_in, queries),
            )
        )
    ]
    for load in loads:
        load.start()
    n_configs, seq = keys.shape[0], keys.shape[1]
    heads, n_cfg = queries.shape[0], arrived.shape[0]
    probe_row = lax.broadcasted_iota(jnp.int32, (heads * 8, seq), 0) & 7
    causal = lax.broadcasted_iota(jnp.int32, (heads * 8, seq), 1) <= seq - 8 + probe_row
    slots = n_cfg * 8
    for load in loads:
        load.wait()
    probes = queries[...].reshape(heads * 8, HD).astype(bf16)
    spliced = arrived[...].astype(f32)
    taken_rows = jnp.concatenate(
        [spliced[:, :8, :].reshape(slots, HD), spliced[:, 8:, :].reshape(slots, HD)], axis=1
    )
    base_all = base_kv[...].astype(f32).reshape(seq, 2 * HD)
    none = jnp.zeros((splices.shape[1] - slots - seq, 2 * HD), f32)
    taken_rows = jnp.concatenate([taken_rows, base_all, none], axis=0).astype(bf16)
    mixed = jnp.dot(splices[...], taken_rows, preferred_element_type=f32)
    for i in range(n_configs):
        row = mixed[i * seq : (i + 1) * seq, :]
        keys[i] = rotate(row[:, :HD], rope[0], rope[1]).astype(bf16)
        values[i] = row[:, HD:].astype(bf16)
    stores = [
        pltpu.make_async_copy(source, target, sem.at[i])
        for i, (source, target) in enumerate(
            ((keys, keys_out), (values, values_out), (attended, attended_out))
        )
    ]
    stores[0].start()
    stores[1].start()
    for i in range(n_configs):
        key, value = keys[i], values[i]
        scores = lax.dot_general(
            probes, key, (((1,), (1,)), ((), ())), preferred_element_type=f32
        ) * HD ** (-0.5)
        scores = jnp.where(causal, scores, -1e30)
        top = jnp.max(scores, axis=1, keepdims=True)
        grown = jnp.exp(scores - top)
        probs = (grown / jnp.sum(grown, axis=1, keepdims=True)).astype(bf16)
        out = jnp.dot(probs, value, preferred_element_type=f32)
        for h in range(heads):
            attended[i, :, h * HD : (h + 1) * HD] = out[h * 8 + 8 - PROBE : h * 8 + 8, :].astype(bf16)
    stores[2].start()
    for store in stores:
        store.wait()


def body(n_cfg, n_tp, pool, base_run, gain, w_key, w_value, w_query, src_pos, dst_pos, counts):
    seq, width = pool.shape[1], pool.shape[2]
    n_configs, cap = dst_pos.shape[0], dst_pos.shape[2]
    heads = w_query.shape[1] // HD
    group = 1 << (n_cfg.bit_length() // 2)
    tile = seq // group
    padded = -(-seq // HD) * HD
    anywhere = pl.BlockSpec(memory_space=pl.ANY)
    dma, hops = pltpu.SemaphoreType.DMA, n_tp - 1
    table = jnp.asarray(rope_tables(0, seq))
    arrived, base_kv, queries, splices = pl.pallas_call(
        functools.partial(sweep_kernel, n_cfg, n_tp),
        out_shape=(
            jax.ShapeDtypeStruct((n_cfg, TILE, HD), bf16),
            jax.ShapeDtypeStruct((group, tile // 8, 8, 2 * HD), bf16),
            jax.ShapeDtypeStruct((heads, 8, HD), f32),
            jax.ShapeDtypeStruct((n_configs * seq, n_cfg * 8 + padded), bf16),
        ),
        in_specs=[anywhere] * 10,
        out_specs=(anywhere,) * 4,
        scratch_shapes=[
            pltpu.SMEM((1,), jnp.int32),
            pltpu.VMEM((n_tp, seq, width), bf16),
            pltpu.VMEM((n_tp * width, 2 * HD), bf16),
            pltpu.VMEM(w_query.shape, bf16),
            pltpu.VMEM((n_cfg, HD), bf16),
            pltpu.VMEM((n_tp, n_cfg // n_tp, HD), f32),
            pltpu.VMEM((cap, n_configs * n_cfg), jnp.int32),
            pltpu.VMEM((n_configs, cap, n_cfg), jnp.int32),
            pltpu.VMEM((n_configs, n_cfg), jnp.int32),
            pltpu.VMEM((2, seq, HD), f32),
            pltpu.VMEM((n_configs * seq, n_cfg * 8 + padded), bf16),
            pltpu.VMEM((group, tile, width), bf16),
            pltpu.VMEM((group, tile, width), bf16),
            pltpu.VMEM((tile // 8, 8, width), bf16),
            pltpu.VMEM((n_cfg // group, 8, width), bf16),
            pltpu.VMEM((n_tp, 8, width), bf16),
            pltpu.VMEM((TILE, width), bf16),
            pltpu.VMEM((n_cfg, TILE, HD), bf16),
            pltpu.VMEM((TILE, HD), bf16),
            pltpu.VMEM((heads, TILE, HD), f32),
            pltpu.VMEM((n_cfg, TILE, HD), f32),
            pltpu.VMEM((8, HD), f32),
            pltpu.VMEM((tile // 8, 8, 2 * HD), bf16),
            pltpu.VMEM((n_cfg * TILE, 2 * padded), bf16),
            pltpu.VMEM((2 * padded, HD), bf16),
            pltpu.VMEM((n_cfg, TILE, HD), bf16),
            pltpu.VMEM((seq, 2 * HD), f32),
            pltpu.VMEM((seq, HD), f32),
            dma((11,)),
            dma((2, hops)),
            dma((2, hops)),
            dma((10,)),
            dma((10,)),
        ],
        compiler_params=pltpu.CompilerParams(
            collective_id=0, has_side_effects=True, vmem_limit_bytes=60 << 20
        ),
    )(
        pool[0],
        base_run,
        gain.reshape(n_cfg, HD),
        w_key,
        w_value,
        w_query,
        jnp.transpose(src_pos[:, 0, :], (1, 0)),
        table,
        jnp.transpose(dst_pos, (0, 2, 1)),
        counts,
    )
    return pl.pallas_call(
        attend_kernel,
        out_shape=(
            jax.ShapeDtypeStruct((n_configs, PROBE, heads * HD), bf16),
            jax.ShapeDtypeStruct((n_configs, seq, HD), bf16),
            jax.ShapeDtypeStruct((n_configs, seq, HD), bf16),
        ),
        in_specs=[anywhere] * 5,
        out_specs=(anywhere,) * 3,
        scratch_shapes=[
            pltpu.VMEM((n_configs, PROBE, heads * HD), bf16),
            pltpu.VMEM((n_configs, seq, HD), bf16),
            pltpu.VMEM((n_configs, seq, HD), bf16),
            pltpu.VMEM(arrived.shape, bf16),
            pltpu.VMEM(base_kv.shape, bf16),
            pltpu.VMEM(queries.shape, f32),
            pltpu.VMEM(splices.shape, bf16),
            pltpu.VMEM(table.shape, f32),
            dma((5,)),
        ],
        compiler_params=pltpu.CompilerParams(vmem_limit_bytes=60 << 20),
    )(arrived, base_kv, queries, splices, table)


def solution(mesh):
    placed = (
        P("cfg", None, "tp"),
        P(),
        P(),
        P(None, "tp"),
        P(None, "tp"),
        P("cfg", "tp"),
        P(None, "cfg", None),
        P("cfg", None, None),
        P("cfg", None),
    )
    return jax.shard_map(
        functools.partial(body, mesh.shape["cfg"], mesh.shape["tp"]),
        mesh=mesh,
        in_specs=placed,
        out_specs=(P("cfg", None, "tp"), P("cfg", None, "tp"), P("cfg", None, "tp")),
        check_vma=False,
    )
```

```python
import functools
import math

import jax
import jax.numpy as jnp
import numpy as np
from jax import lax
from jax.experimental import pallas as pl
from jax.experimental.pallas import tpu as pltpu
from jax.sharding import PartitionSpec as P

HD = 128
PROBE = 4
TILE = 16
ROPE_BASE = 500000.0
EPSILON = 1e-05
MESH = pl.DeviceIdType.MESH
f32 = jnp.float32
bf16 = jnp.bfloat16


def rope_tables(first, count):
    half = HD // 2
    freq = np.exp(np.arange(half, dtype=np.float64) * (-2.0 * math.log(ROPE_BASE) / HD))
    angles = np.arange(first, first + count, dtype=np.float64)[:, None] * freq[None, :]
    cosine, sine = np.cos(angles), np.sin(angles)
    return np.stack(
        [np.concatenate([cosine, cosine], 1), np.concatenate([-sine, sine], 1)]
    ).astype(np.float32)


def rotate(rows, cosine, sine):
    return rows * cosine + pltpu.roll(rows, HD // 2, 1) * sine


def lane_groups(squares):
    total = squares[:, :HD]
    for k in range(1, squares.shape[1] // HD):
        total = total + squares[:, k * HD : (k + 1) * HD]
    return total


def sweep_kernel(
    n_cfg,
    n_tp,
    pool,
    base_run,
    gain,
    w_key,
    w_value,
    w_query,
    src_pos,
    rope_table,
    dst_pos,
    counts,
    arrived,
    base_kv,
    queries,
    splices,
    base,
    rows,
    weights,
    wq,
    gain_raw,
    gain_wide,
    src,
    dst,
    used,
    rope,
    placed,
    masked,
    row_sums,
    middle,
    landed,
    base_rows,
    probe,
    probes_met,
    block,
    part,
    parts,
    my_queries,
    my_base_kv,
    chosen,
    kv,
    outgoing,
    acc,
    sums,
    load_sem,
    ring_send,
    ring_recv,
    send,
    recv,
):
    cfg, tp = lax.axis_index("cfg"), lax.axis_index("tp")
    seq, width = rows.shape[1], rows.shape[2]
    half_rows = seq // 2
    model = n_tp * width
    heads = queries.shape[0]
    group, tile = masked.shape[0], masked.shape[1]
    rings = n_cfg // group
    place, turn = lax.rem(cfg, group), cfg // group
    pieces = tile // 8

    def holder(piece):
        return lax.rem(place + 3 * piece, rings) * group + place

    held = [cfg == holder(piece) for piece in range(pieces)]
    is_holder = functools.reduce(jnp.logical_or, held)
    my_piece = sum(piece * hit.astype(jnp.int32) for piece, hit in enumerate(held))

    def owner(head):
        return (head + rings // 2) % rings * group + head

    is_owner = jnp.logical_and(turn == lax.rem(place + rings // 2, rings), place < heads)
    my_head = lax.rem(place, heads)
    per_plane = n_cfg // n_tp
    makes_block = cfg // per_plane == tp

    loads = [
        pltpu.make_async_copy(source, target, load_sem.at[i])
        for i, (source, target) in enumerate(
            (
                (pool, rows.at[tp]),
                (base_run, base),
                (gain, gain_raw),
                (w_key, weights.at[:, pl.ds(0, HD)]),
                (w_value, weights.at[:, pl.ds(HD, HD)]),
                (w_query, wq),
                (src_pos, src),
                (rope_table, rope),
                (dst_pos, dst),
                (counts, used),
            )
        )
    ]
    for load in loads:
        load.start()

    def outward(i, size):
        step = lax.div(i + 1, 2)
        return lax.rem(size // 2 + jnp.where(lax.rem(i, 2) == 0, step, size - step), size)

    def peer(i):
        across = lax.rem(i, group)
        y = lax.rem(turn + outward(lax.div(i, group), rings), rings)
        x = lax.rem(lax.div(place, 2) + outward(lax.div(across, 2), group // 2), group // 2)
        core = lax.rem(place + 1 - lax.rem(across, 2), 2)
        return y * group + x * 2 + core

    barrier = pltpu.get_barrier_semaphore()

    @pl.loop(1, n_tp)
    def _(i):
        pl.semaphore_signal(
            barrier, inc=1, device_id={"tp": lax.rem(tp + i, n_tp)}, device_id_type=MESH
        )

    @pl.loop(0, n_cfg - 1)
    def _(i):
        pl.semaphore_signal(barrier, inc=1, device_id={"cfg": peer(i)}, device_id_type=MESH)

    loads[0].wait()
    loads[1].wait()
    is_base = jnp.full((tile, width), base[0], jnp.int32) == cfg
    for j in range(group):
        mine = rows[tp, pl.ds(j * tile, tile), :].astype(f32)
        masked[j] = jnp.where(is_base, mine, 0.0).astype(bf16)
    mine = rows[tp, pl.ds(seq - TILE, TILE), :].astype(f32)
    probe[...] = jnp.where(is_base[:TILE, :], mine, 0.0).astype(bf16)
    padded = kv.shape[0] // 2
    cap = src.shape[0]
    n_configs = src.shape[1] // n_cfg

    pl.semaphore_wait(barrier, n_cfg - 1 + n_tp - 1)

    def to_cfg(src, dst, which, target):
        return pltpu.make_async_remote_copy(
            src_ref=src,
            dst_ref=dst,
            send_sem=send.at[which],
            recv_sem=recv.at[which],
            device_id={"cfg": target},
            device_id_type=MESH,
        )

    def both(condition, if_true, if_false):
        pl.when(condition)(if_true)
        pl.when(jnp.logical_not(condition))(if_false)

    def settle(ref, sem):
        pltpu.make_async_copy(ref, ref, sem).wait()

    def ring(direction, unit):
        hop = unit // 2
        part_no = unit % 2 if direction == 0 else 1 - unit % 2
        sign = 1 if direction == 0 else -1
        slot = lax.rem(tp - sign * hop + n_tp, n_tp)
        piece = rows.at[slot, pl.ds(part_no * half_rows, half_rows)]
        return pltpu.make_async_remote_copy(
            src_ref=piece,
            dst_ref=piece,
            send_sem=ring_send.at[direction, unit],
            recv_sem=ring_recv.at[direction, unit],
            device_id={"tp": lax.rem(tp + sign + n_tp, n_tp)},
            device_id_type=MESH,
        )

    def gains(slot):
        eight = gain_wide[slot]
        return jnp.concatenate([eight[k : k + 1, :] for k in range(per_plane)], axis=1)

    def project(slot, part_no, parts_at_once=1):
        piece = pl.ds(part_no * half_rows, half_rows * parts_at_once)
        wide = rows[slot, piece, :].astype(f32)
        sums[piece, :] += lane_groups(wide * wide)
        normed = (wide * gains(slot)).astype(bf16)
        depth = pl.ds(pl.multiple_of(slot * width, width), width)
        acc[piece, :] += jnp.dot(normed, weights[depth, :], preferred_element_type=f32)

    units = n_tp - 1

    def ring_arrives(unit):
        for direction in (0, 1):
            sign = 1 if direction == 0 else -1
            hop = unit // 2 + 1
            part_no = unit % 2 if direction == 0 else 1 - unit % 2
            slot = lax.rem(tp - sign * hop + n_tp, n_tp)
            piece = rows.at[slot, pl.ds(part_no * half_rows, half_rows)]
            pltpu.make_async_copy(piece, piece, ring_recv.at[direction, unit]).wait()
            if unit + 2 < units:
                ring(direction, unit + 2).start()

    def ring_projects(unit):
        if unit == units - 1:
            project(lax.rem(tp + n_tp // 2, n_tp), 0, 2)
            return
        for direction in (0, 1):
            sign = 1 if direction == 0 else -1
            hop = unit // 2 + 1
            part_no = unit % 2 if direction == 0 else 1 - unit % 2
            project(lax.rem(tp - sign * hop + n_tp, n_tp), part_no)

    for k in range(per_plane):

        @pl.when(cfg != tp * per_plane + k)
        def _():
            to_cfg(
                probe.at[:, pl.ds(k * HD, HD)], probes_met.at[cfg], 2, tp * per_plane + k
            ).start()

    for unit in range(min(2, units)):
        ring(0, unit).start()
        ring(1, unit).start()

    @pl.when(makes_block)
    def _():
        lanes = pl.ds(pl.multiple_of(lax.rem(cfg, per_plane) * HD, HD), HD)
        probes_met[cfg] = probe[:, lanes]

    @pl.loop(1, group)
    def _(i):
        other = lax.rem(place + i, group)
        to_cfg(masked.at[other], row_sums.at[place], 0, turn * group + other).start()

    row_sums[place] = masked[place]
    acc[...] = jnp.zeros_like(acc)
    sums[...] = jnp.zeros_like(sums)
    kv[...] = jnp.zeros_like(kv)
    for load in loads[2:]:
        load.wait()
    span_rows = TILE * 4
    config = lax.broadcasted_iota(jnp.int32, (span_rows, src.shape[1]), 1)
    row_no = lax.broadcasted_iota(jnp.int32, (padded, src.shape[1]), 0)
    asked = [(row_no == src[j : j + 1, :]).astype(f32).astype(bf16) for j in range(cap)]
    is_key = lax.broadcasted_iota(jnp.int32, (span_rows, padded), 0) % TILE < 8

    @pl.loop(0, n_cfg // 4)
    def _(i):
        span = pl.ds(pl.multiple_of(i * span_rows, span_rows), span_rows)
        slot = lax.broadcasted_iota(jnp.int32, (span_rows, src.shape[1]), 0)
        target = i * 4 + lax.shift_right_logical(slot, 4)
        slot = slot & 7
        found = jnp.zeros((span_rows, padded), f32)
        for j in range(cap):
            wanted = jnp.zeros(slot.shape, f32)
            for k in range(n_configs):
                hit = jnp.logical_and(config == target * n_configs + k, slot == k * cap + j)
                wanted = wanted + hit.astype(f32)
            found += lax.dot_general(
                wanted.astype(bf16),
                asked[j],
                (((1,), (1,)), ((), ())),
                preferred_element_type=f32,
            )
        chosen[span, pl.ds(0, padded)] = jnp.where(is_key, found, 0.0).astype(bf16)
        chosen[span, pl.ds(padded, padded)] = jnp.where(is_key, 0.0, found).astype(bf16)

    for z in range(n_tp):
        gain_wide[z] = gain_raw[...].astype(f32)[z * per_plane : (z + 1) * per_plane, :]
    project(tp, 0, 2)

    def probes_meet():
        @pl.when(makes_block)
        def _():
            settle(probes_met.at[pl.ds(0, n_cfg - 1)], recv.at[2])

            def add(source, total):
                return total + probes_met[source].astype(f32)

            total = lax.fori_loop(0, n_cfg, add, jnp.zeros((TILE, HD), f32))
            block[...] = total.astype(bf16)

            @pl.loop(1, n_tp)
            def _(i):
                pltpu.make_async_remote_copy(
                    src_ref=block,
                    dst_ref=block,
                    send_sem=send.at[8],
                    recv_sem=recv.at[8],
                    device_id={"tp": lax.rem(tp + i, n_tp)},
                    device_id_type=MESH,
                ).start()

    def base_meets():
        settle(row_sums.at[pl.ds(0, group - 1)], recv.at[0])
        total = row_sums[0].astype(f32)
        for q in range(1, group):
            total += row_sums[q].astype(f32)
        for piece in range(pieces):
            middle[piece] = total[piece * 8 : (piece + 1) * 8, :].astype(bf16)

            @pl.when(jnp.logical_not(held[piece]))
            def _():
                to_cfg(middle.at[piece], landed.at[turn], 7, holder(piece)).start()

            @pl.when(held[piece])
            def _():
                landed[turn] = middle[piece]

    def place_slots():
        slots = n_cfg * 8
        source = lax.broadcasted_iota(jnp.int32, (n_cfg, slots), 0)
        slot = lax.broadcasted_iota(jnp.int32, (n_cfg, slots), 1)
        spread = (source == lax.shift_right_logical(slot, 3)).astype(f32).astype(bf16)
        position = lax.broadcasted_iota(jnp.int32, (seq, slots), 0).astype(f32) + 1.0
        slot_of = lax.broadcasted_iota(jnp.int32, (8, slots), 1) & 7
        row_id = lax.broadcasted_iota(jnp.int32, (8, slots), 0)
        order = lax.broadcasted_iota(jnp.int32, (cap, n_cfg), 0)
        down = lax.broadcasted_iota(jnp.int32, (seq, padded), 0)
        diagonal = (down == lax.broadcasted_iota(jnp.int32, (seq, padded), 1)).astype(f32)
        for i in range(n_configs):
            valid = order < used[i : i + 1, :]
            goal = jnp.where(valid, dst[i] + 1, 0).astype(f32)
            goal = jnp.concatenate([goal, jnp.zeros((8 - cap, n_cfg), f32)], axis=0)
            wide = jnp.dot(goal.astype(bf16), spread, preferred_element_type=f32)
            mine = jnp.logical_and(slot_of == row_id + i * cap, row_id < cap)
            goal = jnp.sum(jnp.where(mine, wide, 0.0), axis=0, keepdims=True)
            onehot = (position == goal).astype(f32)
            free = 1.0 - jnp.max(onehot, axis=1, keepdims=True)
            placed[pl.ds(i * seq, seq), pl.ds(0, slots)] = onehot.astype(bf16)
            placed[pl.ds(i * seq, seq), pl.ds(slots, padded)] = (diagonal * free).astype(bf16)
        pltpu.make_async_copy(placed, splices, load_sem.at[3]).start()

    def base_arrives():
        @pl.when(is_holder)
        def _():
            settle(landed.at[pl.ds(0, rings - 1)], recv.at[7])
            total = landed[0].astype(f32)
            for y in range(1, rings):
                total += landed[y].astype(f32)
            base_rows[tp] = total.astype(bf16)

            @pl.loop(1, n_tp)
            def _(i):
                pltpu.make_async_remote_copy(
                    src_ref=base_rows.at[tp],
                    dst_ref=base_rows.at[tp],
                    send_sem=send.at[1],
                    recv_sem=recv.at[1],
                    device_id={"tp": lax.rem(tp + i, n_tp)},
                    device_id_type=MESH,
                ).start()

    def base_projects():
        @pl.when(is_holder)
        def _():
            settle(base_rows.at[pl.ds(0, n_tp - 1)], recv.at[1])

            def add(z, state):
                total, squares = state
                wide = base_rows[z].astype(f32)
                normed = (wide * gains(z)).astype(bf16)
                depth = pl.ds(pl.multiple_of(z * width, width), width)
                total += jnp.dot(normed, weights[depth, :], preferred_element_type=f32)
                return total, squares + lane_groups(wide * wide)

            total, squares = lax.fori_loop(
                0, n_tp, add, (jnp.zeros((8, 2 * HD), f32), jnp.zeros((8, HD), f32))
            )
            scale = lax.rsqrt(jnp.sum(squares, axis=1, keepdims=True) / model + EPSILON)
            my_base_kv[my_piece] = (total * scale).astype(bf16)

            @pl.loop(0, rings - 1)
            def _(i):
                other = lax.rem(turn + outward(i, rings), rings)
                mine = my_base_kv.at[my_piece]
                to_cfg(mine, mine, 3, other * group + place).start()

    def base_spreads():
        both(
            is_holder,
            lambda: settle(my_base_kv.at[pl.ds(0, pieces - 1)], recv.at[3]),
            lambda: settle(my_base_kv, recv.at[3]),
        )

        @pl.loop(1, group)
        def _(i):
            other = lax.rem(place + i, group)
            to_cfg(my_base_kv, base_kv.at[place], 9, turn * group + other).start()

        pltpu.make_async_copy(my_base_kv, base_kv.at[place], load_sem.at[0]).start()

    def query_parts():
        @pl.when(jnp.logical_not(makes_block))
        def _():
            settle(block, recv.at[8])

        wide = block[...].astype(f32)[TILE - 8 :, :]
        own_gain = gain_wide[cfg // per_plane]
        pick = lax.broadcasted_iota(jnp.int32, own_gain.shape, 0) == lax.rem(cfg, per_plane)
        own_gain = jnp.sum(jnp.where(pick, own_gain, 0.0), axis=0, keepdims=True)
        normed = (wide * own_gain).astype(bf16)
        total = jnp.dot(normed, wq[...], preferred_element_type=f32)
        squares = wide * wide
        for h in range(heads):
            part[h, pl.ds(0, 8), :] = total[:, h * HD : (h + 1) * HD]
            part[h, pl.ds(8, 8), :] = squares
        for h in range(heads):

            @pl.when(cfg != owner(h))
            def _():
                to_cfg(part.at[h], parts.at[cfg], 4, owner(h)).start()

        @pl.when(is_owner)
        def _():
            parts[cfg] = part[my_head]

    def query_sums():
        @pl.when(is_owner)
        def _():
            settle(parts.at[pl.ds(0, n_cfg - 1)], recv.at[4])

            def add(s, total):
                return total + parts[s]

            total = lax.fori_loop(0, n_cfg, add, jnp.zeros((TILE, HD), f32))
            scale = lax.rsqrt(jnp.sum(total[8:], axis=1, keepdims=True) / model + EPSILON)
            my_queries[...] = rotate(
                total[:8] * scale, rope[0, pl.ds(seq - 8, 8), :], rope[1, pl.ds(seq - 8, 8), :]
            )


            @pl.loop(0, rings - 1)
            def _(i):
                other = lax.rem(turn + outward(i, rings), rings)
                to_cfg(my_queries, my_queries, 5, other * group + place).start()

    passes_on = place < heads

    def query_spreads():
        @pl.when(jnp.logical_and(passes_on, jnp.logical_not(is_owner)))
        def _():
            settle(my_queries, recv.at[5])

        @pl.when(passes_on)
        def _():
            pltpu.make_async_copy(my_queries, queries.at[my_head], load_sem.at[1]).start()

            @pl.loop(1, group)
            def _(i):
                other = lax.rem(place + i, group)
                to_cfg(my_queries, queries.at[my_head], 10, turn * group + other).start()

    beside = [
        (probes_meet, base_meets),
        (base_arrives, query_parts),
        (base_projects,),
        (query_sums,),
        (base_spreads,),
        (query_spreads, place_slots),
    ]
    for unit in range(max(units, len(beside))):
        if unit < units:
            ring_arrives(unit)
        if unit < len(beside):
            for stage in beside[unit]:
                stage()
        if unit < units:
            ring_projects(unit)

    scale = lax.rsqrt(jnp.sum(sums[...], axis=1, keepdims=True) / model + EPSILON)
    scaled = (acc[...] * scale).astype(bf16)
    kv[pl.ds(0, seq), :] = scaled[:, :HD]
    kv[pl.ds(padded, seq), :] = scaled[:, HD:]

    @pl.loop(0, rings)
    def _(step):
        first = lax.rem(turn + outward(step, rings), rings) * group
        span = pl.ds(pl.multiple_of(first * TILE, TILE * group), TILE * group)
        picked = jnp.dot(chosen[span, :], kv[...], preferred_element_type=f32).astype(bf16)
        outgoing[pl.ds(first, group)] = picked.reshape(group, TILE, HD)

        @pl.loop(0, group)
        def _(across):
            x = lax.rem(lax.div(place, 2) + outward(lax.div(across, 2), group // 2), group // 2)
            target = first + x * 2 + lax.rem(place + 1 - lax.rem(across, 2), 2)

            @pl.when(target != cfg)
            def _():
                to_cfg(outgoing.at[target], arrived.at[cfg], 6, target).start()

    own = pltpu.make_async_copy(outgoing.at[cfg], arrived.at[cfg], load_sem.at[2])
    own.start()

    for unit in range(units):
        for direction in (0, 1):
            ring(direction, unit).wait_send()
    settle(masked.at[pl.ds(0, group - 1)], send.at[0])

    both(
        is_holder,
        lambda: settle(middle.at[pl.ds(0, pieces - 1)], send.at[7]),
        lambda: settle(middle, send.at[7]),
    )

    @pl.when(is_holder)
    def _():
        settle(base_rows.at[pl.ds(0, n_tp - 1)], send.at[1])
        settle(base_kv.at[pl.ds(0, rings - 1), 0], send.at[3])

    both(
        makes_block,
        lambda: settle(probes_met.at[pl.ds(0, per_plane - 1)], send.at[2]),
        lambda: settle(probes_met.at[pl.ds(0, per_plane)], send.at[2]),
    )

    @pl.when(makes_block)
    def _():
        settle(probes_met.at[pl.ds(0, n_tp - 1)], send.at[8])

    both(
        is_owner,
        lambda: settle(part.at[pl.ds(0, heads - 1)], send.at[4]),
        lambda: settle(part, send.at[4]),
    )
    settle(base_kv.at[pl.ds(0, group - 1)], send.at[9])
    settle(base_kv.at[pl.ds(0, group - 1)], recv.at[9])
    both(
        passes_on,
        lambda: settle(queries.at[pl.ds(0, heads - 1)], recv.at[10]),
        lambda: settle(queries, recv.at[10]),
    )

    @pl.when(is_owner)
    def _():
        settle(arrived.at[pl.ds(0, rings - 1)], send.at[5])

    @pl.when(passes_on)
    def _():
        settle(arrived.at[pl.ds(0, group - 1)], send.at[10])

    settle(outgoing.at[pl.ds(0, n_cfg - 1)], send.at[6])
    settle(arrived.at[pl.ds(0, n_cfg - 1)], recv.at[6])
    own.wait()
    pltpu.make_async_copy(placed, splices, load_sem.at[3]).wait()

    pltpu.make_async_copy(my_base_kv, base_kv.at[place], load_sem.at[0]).wait()

    @pl.when(passes_on)
    def _():
        pltpu.make_async_copy(my_queries, queries.at[my_head], load_sem.at[1]).wait()


def attend_kernel(
    arrived_in,
    base_in,
    queries_in,
    splices_in,
    rope_in,
    attended_out,
    keys_out,
    values_out,
    attended,
    keys,
    values,
    arrived,
    base_kv,
    queries,
    splices,
    rope,
    sem,
):
    loads = [
        pltpu.make_async_copy(source, target, sem.at[i])
        for i, (source, target) in enumerate(
            (
                (splices_in, splices),
                (arrived_in, arrived),
                (base_in, base_kv),
                (rope_in, rope),
                (queries_in, queries),
            )
        )
    ]
    for load in loads:
        load.start()
    n_configs, seq = keys.shape[0], keys.shape[1]
    heads, n_cfg = queries.shape[0], arrived.shape[0]
    probe_row = lax.broadcasted_iota(jnp.int32, (heads * 8, seq), 0) & 7
    causal = lax.broadcasted_iota(jnp.int32, (heads * 8, seq), 1) <= seq - 8 + probe_row
    slots = n_cfg * 8
    for load in loads:
        load.wait()
    probes = queries[...].reshape(heads * 8, HD).astype(bf16)
    spliced = arrived[...].astype(f32)
    taken_rows = jnp.concatenate(
        [spliced[:, :8, :].reshape(slots, HD), spliced[:, 8:, :].reshape(slots, HD)], axis=1
    )
    base_all = base_kv[...].astype(f32).reshape(seq, 2 * HD)
    none = jnp.zeros((splices.shape[1] - slots - seq, 2 * HD), f32)
    taken_rows = jnp.concatenate([taken_rows, base_all, none], axis=0).astype(bf16)
    mixed = jnp.dot(splices[...], taken_rows, preferred_element_type=f32)
    for i in range(n_configs):
        row = mixed[i * seq : (i + 1) * seq, :]
        keys[i] = rotate(row[:, :HD], rope[0], rope[1]).astype(bf16)
        values[i] = row[:, HD:].astype(bf16)
    stores = [
        pltpu.make_async_copy(source, target, sem.at[i])
        for i, (source, target) in enumerate(
            ((keys, keys_out), (values, values_out), (attended, attended_out))
        )
    ]
    stores[0].start()
    stores[1].start()
    for i in range(n_configs):
        key, value = keys[i], values[i]
        scores = lax.dot_general(
            probes, key, (((1,), (1,)), ((), ())), preferred_element_type=f32
        ) * HD ** (-0.5)
        scores = jnp.where(causal, scores, -1e30)
        top = jnp.max(scores, axis=1, keepdims=True)
        grown = jnp.exp(scores - top)
        probs = (grown / jnp.sum(grown, axis=1, keepdims=True)).astype(bf16)
        out = jnp.dot(probs, value, preferred_element_type=f32)
        for h in range(heads):
            attended[i, :, h * HD : (h + 1) * HD] = out[h * 8 + 8 - PROBE : h * 8 + 8, :].astype(bf16)
    stores[2].start()
    for store in stores:
        store.wait()


def body(n_cfg, n_tp, pool, base_run, gain, w_key, w_value, w_query, src_pos, dst_pos, counts):
    seq, width = pool.shape[1], pool.shape[2]
    n_configs, cap = dst_pos.shape[0], dst_pos.shape[2]
    heads = w_query.shape[1] // HD
    group = 1 << (n_cfg.bit_length() // 2)
    tile = seq // group
    padded = -(-seq // HD) * HD
    anywhere = pl.BlockSpec(memory_space=pl.ANY)
    dma, hops = pltpu.SemaphoreType.DMA, n_tp - 1
    table = jnp.asarray(rope_tables(0, seq))
    arrived, base_kv, queries, splices = pl.pallas_call(
        functools.partial(sweep_kernel, n_cfg, n_tp),
        out_shape=(
            jax.ShapeDtypeStruct((n_cfg, TILE, HD), bf16),
            jax.ShapeDtypeStruct((group, tile // 8, 8, 2 * HD), bf16),
            jax.ShapeDtypeStruct((heads, 8, HD), f32),
            jax.ShapeDtypeStruct((n_configs * seq, n_cfg * 8 + padded), bf16),
        ),
        in_specs=[anywhere] * 10,
        out_specs=(anywhere,) * 4,
        scratch_shapes=[
            pltpu.SMEM((1,), jnp.int32),
            pltpu.VMEM((n_tp, seq, width), bf16),
            pltpu.VMEM((n_tp * width, 2 * HD), bf16),
            pltpu.VMEM(w_query.shape, bf16),
            pltpu.VMEM((n_cfg, HD), bf16),
            pltpu.VMEM((n_tp, n_cfg // n_tp, HD), f32),
            pltpu.VMEM((cap, n_configs * n_cfg), jnp.int32),
            pltpu.VMEM((n_configs, cap, n_cfg), jnp.int32),
            pltpu.VMEM((n_configs, n_cfg), jnp.int32),
            pltpu.VMEM((2, seq, HD), f32),
            pltpu.VMEM((n_configs * seq, n_cfg * 8 + padded), bf16),
            pltpu.VMEM((group, tile, width), bf16),
            pltpu.VMEM((group, tile, width), bf16),
            pltpu.VMEM((tile // 8, 8, width), bf16),
            pltpu.VMEM((n_cfg // group, 8, width), bf16),
            pltpu.VMEM((n_tp, 8, width), bf16),
            pltpu.VMEM((TILE, width), bf16),
            pltpu.VMEM((n_cfg, TILE, HD), bf16),
            pltpu.VMEM((TILE, HD), bf16),
            pltpu.VMEM((heads, TILE, HD), f32),
            pltpu.VMEM((n_cfg, TILE, HD), f32),
            pltpu.VMEM((8, HD), f32),
            pltpu.VMEM((tile // 8, 8, 2 * HD), bf16),
            pltpu.VMEM((n_cfg * TILE, 2 * padded), bf16),
            pltpu.VMEM((2 * padded, HD), bf16),
            pltpu.VMEM((n_cfg, TILE, HD), bf16),
            pltpu.VMEM((seq, 2 * HD), f32),
            pltpu.VMEM((seq, HD), f32),
            dma((11,)),
            dma((2, hops)),
            dma((2, hops)),
            dma((11,)),
            dma((11,)),
        ],
        compiler_params=pltpu.CompilerParams(
            collective_id=0, has_side_effects=True, vmem_limit_bytes=60 << 20
        ),
    )(
        pool[0],
        base_run,
        gain.reshape(n_cfg, HD),
        w_key,
        w_value,
        w_query,
        jnp.transpose(src_pos[:, 0, :], (1, 0)),
        table,
        jnp.transpose(dst_pos, (0, 2, 1)),
        counts,
    )
    return pl.pallas_call(
        attend_kernel,
        out_shape=(
            jax.ShapeDtypeStruct((n_configs, PROBE, heads * HD), bf16),
            jax.ShapeDtypeStruct((n_configs, seq, HD), bf16),
            jax.ShapeDtypeStruct((n_configs, seq, HD), bf16),
        ),
        in_specs=[anywhere] * 5,
        out_specs=(anywhere,) * 3,
        scratch_shapes=[
            pltpu.VMEM((n_configs, PROBE, heads * HD), bf16),
            pltpu.VMEM((n_configs, seq, HD), bf16),
            pltpu.VMEM((n_configs, seq, HD), bf16),
            pltpu.VMEM(arrived.shape, bf16),
            pltpu.VMEM(base_kv.shape, bf16),
            pltpu.VMEM(queries.shape, f32),
            pltpu.VMEM(splices.shape, bf16),
            pltpu.VMEM(table.shape, f32),
            dma((5,)),
        ],
        compiler_params=pltpu.CompilerParams(vmem_limit_bytes=60 << 20),
    )(arrived, base_kv, queries, splices, table)


def solution(mesh):
    placed = (
        P("cfg", None, "tp"),
        P(),
        P(),
        P(None, "tp"),
        P(None, "tp"),
        P("cfg", "tp"),
        P(None, "cfg", None),
        P("cfg", None, None),
        P("cfg", None),
    )
    return jax.shard_map(
        functools.partial(body, mesh.shape["cfg"], mesh.shape["tp"]),
        mesh=mesh,
        in_specs=placed,
        out_specs=(P("cfg", None, "tp"), P("cfg", None, "tp"), P("cfg", None, "tp")),
        check_vma=False,
    )
```
